256 devices in a mesh: ctx: 16 (over x_lo, y, core), ch: 16 (over x_hi, z).
Axes of the slice: x: 4 (x_hi: 2, x_lo: 2; x = x_hi * 2 + x_lo), y: 4, z: 8, core: 2. Of those that a mesh axis runs over, the one named last changes fastest.
Arguments:
- inputs: bfloat16 [1024, 32768], P('ch', 'ctx'), may hold values from -6 to 6
- cotangent: bfloat16 [1024, 32768], P('ch', 'ctx'), may hold values from -0.03125 to 0.03125
- features: float32 [64, 4096], P(None, 'ctx'), may hold values from -6 to 6
- projection: float32 [64, 1024], P(None, 'ch'), may hold values from -0.75 to 0.75
- decay_rates: float32 [1024], P('ch'), may hold values from 0.5 to 8
Outputs:
- x_grad: bfloat16 [1024, 32768], P('ch', 'ctx')
- filter_grad: float32 [1024, 4096], P('ch', 'ctx')
- feature_grad: float32 [64, 4096], P(None, 'ctx')
The draws below stay inside these ranges and needn't reach their ends.
All inputs are finite; a program needn't handle non-finite values.
Results may differ from the reference program's by a relative error of at most 0.001.
Values may be sent and summed in bfloat16 or wider, within the bound.
No kernel may reach another device: no remote copies, remote signals or barrier semaphores. Data moves between devices by JAX's collectives and lax.ppermute only.
A program may use at most 128 MiB of HBM per device.

```python
import math
import jax
import jax.numpy as jnp
from jax import lax

CHANNELS = 1024
ORDER = 64
TAPS = 4096
TOKENS = 32768


def steps_of(own_key, shape, pieces, smallest, high):
    loudness = 1.0
    for dim, parts in pieces:
        heights = jax.random.uniform(jax.random.fold_in(jax.random.fold_in(own_key, 6), dim), (parts,), jnp.float32, smallest / len(pieces), high / len(pieces))
        loudness = loudness * jnp.repeat(jnp.exp(heights), shape[dim] // parts).reshape((-1,) + (1,) * (len(shape) - 1 - dim))
    return loudness


def normal_values(rng, shape, width, most, pieces=(), dtype=jnp.bfloat16):
    entries = width * jax.random.normal(rng, shape, jnp.float32)
    if pieces:
        entries = entries * steps_of(rng, shape, pieces, -0.22, 0.18)
    return jnp.clip(entries, -most, most).astype(dtype)


def setup_inputs(seed: int = 0) -> dict:
    keys = jax.random.split(jax.random.key(seed), 6)
    return {
        "inputs": normal_values(keys[0], (CHANNELS, TOKENS), 1.0, 6.0, ((0, 16), (1, 16))),
        "cotangent": normal_values(keys[1], (CHANNELS, TOKENS), TOKENS ** -0.5, 0.03125, ((0, 16), (1, 16))),
        "features": normal_values(keys[2], (ORDER, TAPS), 1.0, 6.0, ((1, 16),), jnp.float32),
        "projection": normal_values(keys[3], (ORDER, CHANNELS), ORDER ** -0.5, 0.75, ((1, 16),), jnp.float32),
        "decay_rates": jnp.clip(jnp.exp(math.log(8.0) - 2.7725887 * jax.random.uniform(keys[4], (CHANNELS,), jnp.float32) ** steps_of(keys[4], (CHANNELS,), ((0, 16),), -0.2, 0.2)), 0.5, 8.0),
    }


def reference(inputs, cotangent, features, projection, decay_rates):
    highest = lax.Precision.HIGHEST
    positions = jnp.arange(TAPS).astype(jnp.float32)
    decay_factor = jnp.exp(-decay_rates[None, :] * (positions[:, None] / TAPS))
    filters = decay_factor * jnp.dot(features.T, projection, precision=highest)
    signal = inputs.astype(jnp.float32).T
    grad_out = cotangent.astype(jnp.float32).T
    fft_len = TOKENS + TAPS
    spectrum_cot = jnp.fft.rfft(grad_out[::-1], n=fft_len, axis=0)
    correlated = jnp.fft.irfft(jnp.fft.rfft(filters, n=fft_len, axis=0) * spectrum_cot, n=fft_len, axis=0)
    x_grad = correlated[:TOKENS][::-1].T.astype(jnp.bfloat16)
    cross_corr = jnp.fft.irfft(spectrum_cot * jnp.fft.rfft(signal, n=fft_len, axis=0), n=fft_len, axis=0)
    filter_grad = cross_corr[TOKENS - TAPS:TOKENS][::-1]
    feature_grad = jnp.dot(projection, (decay_factor * filter_grad).T, precision=highest)
    return x_grad, filter_grad.T, feature_grad
```

```python
import math

import jax
import jax.numpy as jnp
import numpy as np
from jax import lax
from jax.experimental import pallas as pl
from jax.experimental.pallas import tpu as pltpu
from jax.sharding import PartitionSpec as P

SUB = 256
LANES = 128
F32 = jnp.float32
BF16 = jnp.bfloat16
VMEM_LIMIT = 40 * 1024 * 1024


def dft_tables():
    order = np.concatenate([np.arange(0, SUB, 2), np.arange(1, SUB, 2)])
    angles = 2.0 * np.pi * np.arange(SUB)[:, None] * (order[None, :] + 0.5) / (2 * SUB)
    forward = np.concatenate([np.cos(angles), -np.sin(angles)], axis=1)
    pair = []
    for table in (forward, forward.T / SUB):
        high = table.astype(jnp.bfloat16)
        low = (table - high.astype(np.float64)).astype(jnp.bfloat16)
        pair.append(jnp.asarray(np.stack([high, low])))
    return pair


def dot(left, right):
    return jnp.dot(left, right, preferred_element_type=F32)


def two_terms(values):
    high = values.astype(BF16)
    return high, (values - high.astype(F32)).astype(BF16)


def dot_terms(values, table):
    high, low = two_terms(values)
    return dot(high, table[0]) + dot(high, table[1]) + dot(low, table[0])


def pack_kernel(groups, taps, cot_ref, in_ref, feat_ref, proj_ref, rate_ref, pay_ref, decay_ref, rows, frows):
    channels, block_len = cot_ref.shape
    per = channels // groups
    subs = block_len // SUB
    for which, ref in enumerate((cot_ref, in_ref)):
        for sub in range(subs):
            for half in range(2):
                start = sub * SUB + half * LANES
                rows[2 * which + half, pl.ds(sub, channels, stride=subs), :] = ref[:, start : start + LANES].astype(F32)
    span = per * subs
    for part in range(4):
        for group in range(groups):
            pay_ref[group, part * span : (part + 1) * span, :] = rows[part, group * span : (group + 1) * span, :].astype(BF16)
    tap_rows = feat_ref.shape[1]
    first = lax.axis_index("ctx") * tap_rows
    positions = (first + lax.broadcasted_iota(jnp.int32, (1, tap_rows), 1)).astype(F32)
    diagonal = lax.broadcasted_iota(jnp.int32, (channels, channels), 0) == lax.broadcasted_iota(
        jnp.int32, (channels, channels), 1
    )
    rates = jnp.sum(jnp.where(diagonal, rate_ref[...], 0.0), axis=1, keepdims=True)
    decay = jnp.exp(-rates * (positions / taps))
    decay_ref[...] = decay
    product = lax.dot_general(
        proj_ref[...],
        feat_ref[...],
        (((0,), (0,)), ((), ())),
        precision=lax.Precision.HIGHEST,
        preferred_element_type=F32,
    )
    high, low = two_terms(decay * product)
    high = high.astype(F32)
    low = low.astype(F32)
    for group in range(groups):
        own = slice(group * per, (group + 1) * per)
        for half in range(2):
            lanes = slice(half * LANES, (half + 1) * LANES)
            base = half * 2 * per
            frows[group, base : base + per, :] = high[own, lanes]
            frows[group, base + per : base + 2 * per, :] = low[own, lanes]
    pay_ref[:, 4 * span :, :] = frows[...].astype(BF16)


def block_spectra(recv_ref, base, table_ref, store):
    groups = recv_ref.shape[0]
    span = 32
    per, subs = 4, 8
    step = 4
    for first in range(0, groups, step):
        halves = [
            recv_ref[first : first + step, base + half * span : base + (half + 1) * span, :].reshape(step * span, LANES)
            for half in range(2)
        ]
        left = jnp.concatenate(halves, axis=1)
        result = dot(left, table_ref[0]) + dot(left, table_ref[1])
        for src in range(step):
            for chan in range(per):
                row = (src * per + chan) * subs
                for tile in range(4):
                    store(chan, tile, (first + src) * subs, result[row : row + subs, tile * LANES : (tile + 1) * LANES])


def taps_kernel(recv_ref, fwd_ref, inv_ref, win_ref, grad_ref, cot_spec, in_spec, sums, spec):
    groups = recv_ref.shape[0]
    per, subs, lags = 4, 8, 16
    blocks = groups * subs

    def store_cot(chan, tile, row, value):
        cot_spec[chan, tile, row : row + subs, :] = value

    def store_in(chan, tile, row, value):
        in_spec[chan, tile, row : row + subs, :] = value

    block_spectra(recv_ref, 0, fwd_ref, store_cot)
    cot_spec[:, :, blocks:, :] = jnp.zeros((per, 4, subs, LANES), F32)
    block_spectra(recv_ref, 64, fwd_ref, store_in)
    win_ref[:, :, blocks:, :] = jnp.zeros((per, 4, lags, LANES), F32)
    for chan in range(per):
        now = [cot_spec[chan, tile, 0:blocks, :] for tile in range(4)]
        nxt = [cot_spec[chan, tile, 1 : blocks + 1, :] for tile in range(4)]
        win_ref[chan, 0, 0:blocks, :] = now[0] + nxt[2]
        win_ref[chan, 1, 0:blocks, :] = now[1] - nxt[3]
        win_ref[chan, 2, 0:blocks, :] = now[2] - nxt[0]
        win_ref[chan, 3, 0:blocks, :] = now[3] + nxt[1]

    def one(index, carry):
        chan = index // 2
        half = index % 2
        acc_re = [None] * lags
        acc_im = [None] * lags
        for src in range(groups):
            left_re = in_spec[chan, half, src * subs : (src + 1) * subs, :]
            left_im = in_spec[chan, 2 + half, src * subs : (src + 1) * subs, :]
            for lag in range(lags):
                row = src * subs + lag
                win_re = win_ref[chan, half, row : row + subs, :]
                win_im = win_ref[chan, 2 + half, row : row + subs, :]
                term_re = left_re * win_re + left_im * win_im
                term_im = left_re * win_im - left_im * win_re
                acc_re[lag] = term_re if src == 0 else acc_re[lag] + term_re
                acc_im[lag] = term_im if src == 0 else acc_im[lag] + term_im
        for part, acc in enumerate((acc_re, acc_im)):
            for lag in range(lags):
                sums[part, lag * subs : (lag + 1) * subs, :] = acc[lag]
            total = sums[part, pl.ds(0, lags, stride=subs), :]
            for sub in range(1, subs):
                total = total + sums[part, pl.ds(sub, lags, stride=subs), :]
            spec[2 * part + half, pl.ds(chan, lags, stride=per), :] = total
        return carry

    lax.fori_loop(0, 2 * per, one, 0)
    left = jnp.concatenate([spec[tile] for tile in range(4)], axis=1)
    result = dot_terms(left, inv_ref)
    for lag in range(lags):
        own = slice(lag * per, (lag + 1) * per)
        grad_ref[lag, 0:per, :] = result[own, 0:LANES]
        grad_ref[lag, per : 2 * per, :] = result[own, LANES:]


def inputs_kernel(recv_ref, win_ref, fwd_ref, inv_ref, grad_ref, frows, fspec, spec):
    groups = recv_ref.shape[0]
    per, subs, lags = 4, 8, 16
    blocks = groups * subs
    frows[...] = recv_ref[:, 128:144, :].astype(F32).reshape(groups * 16, LANES)
    terms = []
    for term in range(2):
        chans = []
        for chan in range(per):
            halves = [frows[pl.ds(half * 2 * per + term * per + chan, lags, stride=16), :] for half in range(2)]
            chans.append(jnp.concatenate(halves, axis=1))
        terms.append(jnp.concatenate(chans, axis=0).astype(BF16))
    result = dot(terms[0], fwd_ref[0]) + dot(terms[0], fwd_ref[1]) + dot(terms[1], fwd_ref[0])
    for tile in range(4):
        for chan in range(per):
            fspec[chan, tile] = result[chan * lags : (chan + 1) * lags, tile * LANES : (tile + 1) * LANES]

    def one(index, carry):
        chan = index // 2
        half = index % 2
        filt_re = [jnp.broadcast_to(fspec[chan, half, lag : lag + 1, :], (subs, LANES)) for lag in range(lags)]
        filt_im = [jnp.broadcast_to(fspec[chan, 2 + half, lag : lag + 1, :], (subs, LANES)) for lag in range(lags)]
        for src in range(groups):
            acc_re = None
            acc_im = None
            for lag in range(lags):
                row = src * subs + lag
                win_re = win_ref[chan, half, row : row + subs, :]
                win_im = win_ref[chan, 2 + half, row : row + subs, :]
                term_re = filt_re[lag] * win_re + filt_im[lag] * win_im
                term_im = filt_re[lag] * win_im - filt_im[lag] * win_re
                acc_re = term_re if lag == 0 else acc_re + term_re
                acc_im = term_im if lag == 0 else acc_im + term_im
            spec[chan, half, src * subs : (src + 1) * subs, :] = acc_re
            spec[chan, 2 + half, src * subs : (src + 1) * subs, :] = acc_im
        return carry

    lax.fori_loop(0, 2 * per, one, 0)
    for first in range(0, per, 2):
        pair = []
        for chan in (first, first + 1):
            left = jnp.concatenate([spec[chan, tile] for tile in range(4)], axis=1)
            pair.append(dot_terms(left, inv_ref).reshape(groups, subs, SUB))
        both = jnp.concatenate(pair, axis=1)
        grad_ref[:, first * subs : (first + 2) * subs, :] = both.astype(BF16)


def features_kernel(grad_ref, decay_ref, proj_ref, out_ref, part_ref):
    groups = grad_ref.shape[0]
    per = grad_ref.shape[1] // 2
    for group in range(groups):
        own = slice(group * per, (group + 1) * per)
        out_ref[own, 0:LANES] = grad_ref[group, 0:per, :]
        out_ref[own, LANES:] = grad_ref[group, per : 2 * per, :]
    part_ref[...] = jnp.dot(
        proj_ref[...],
        decay_ref[...] * out_ref[...],
        precision=lax.Precision.HIGHEST,
        preferred_element_type=F32,
    )


def call(kernel, out, scratch, flops):
    return pl.pallas_call(
        kernel,
        out_shape=out,
        scratch_shapes=[pltpu.VMEM(shape, F32) for shape in scratch],
        compiler_params=pltpu.CompilerParams(vmem_limit_bytes=VMEM_LIMIT),
        cost_estimate=pl.CostEstimate(flops=flops, bytes_accessed=1 << 20, transcendentals=0),
    )


def shifted(values, axis, distance, ring):
    size = lax.axis_size(axis)
    route = [(i, i - i % ring + (i + distance) % ring) for i in range(size)]
    return lax.ppermute(values, axis, route)


def summed(values, axis):
    size = lax.axis_size(axis)
    half = size // 2
    values = values + lax.ppermute(values, axis, [(i, (i + half) % size) for i in range(size)])
    below = shifted(values, axis, 1, half)
    above = shifted(values, axis, -1, half)
    two = values + above
    three = two + below
    return three + shifted(three, axis, -3, half) + shifted(two, axis, 3, half)


def shards(inputs, cotangent, features, projection, decay_rates):
    channels, block_len = inputs.shape
    tap_rows = features.shape[1]
    groups = lax.axis_size("ctx")
    per = channels // groups
    subs = block_len // SUB
    taps = 2 * block_len
    lags = taps // SUB
    shape = jax.ShapeDtypeStruct
    forward, backward = dft_tables()

    def exchanged(values):
        return lax.all_to_all(values, "ctx", 0, 0, tiled=True)

    payload, decay = call(
        lambda *refs: pack_kernel(groups, taps, *refs),
        (shape((groups, 144, LANES), BF16), shape((channels, tap_rows), F32)),
        [(4, channels * subs, LANES), (groups, 16, LANES)],
        1 << 22,
    )(cotangent, inputs, features, projection, decay_rates.reshape(1, channels))
    received = exchanged(payload)
    blocks = groups * subs
    windows, tap_grads = call(
        taps_kernel,
        (shape((per, 4, blocks + lags, LANES), F32), shape((groups, 2 * per, LANES), F32)),
        [(per, 4, blocks + subs, LANES), (per, 4, blocks, LANES), (2, lags * subs, LANES), (4, per * lags, LANES)],
        1 << 32,
    )(received, forward, backward)
    tap_grads = exchanged(tap_grads)
    x_parts = call(
        inputs_kernel,
        shape((groups, per * subs, SUB), BF16),
        [(groups * 16, LANES), (per, 4, lags, LANES), (per, 4, blocks, LANES)],
        1 << 32,
    )(received, windows, forward, backward)
    x_grad = exchanged(x_parts).reshape(channels, block_len)
    filter_grad, part = call(
        features_kernel,
        (shape((channels, tap_rows), F32), shape((projection.shape[0], tap_rows), F32)),
        [],
        1 << 22,
    )(tap_grads, decay, projection)
    feature_grad = summed(part, "ch")
    return (x_grad, filter_grad, feature_grad)


def solution(mesh):
    placed = (P("ch", "ctx"), P("ch", "ctx"), P(None, "ctx"), P(None, "ch"), P("ch"))
    return jax.shard_map(
        shards,
        mesh=mesh,
        in_specs=placed,
        out_specs=(P("ch", "ctx"), P("ch", "ctx"), P(None, "ctx")),
        check_vma=False,
    )
```

```python
import math

import jax
import jax.numpy as jnp
import numpy as np
from jax import lax
from jax.experimental import pallas as pl
from jax.experimental.pallas import tpu as pltpu
from jax.sharding import PartitionSpec as P

SUB = 256
LANES = 128
F32 = jnp.float32
BF16 = jnp.bfloat16
VMEM_LIMIT = 40 * 1024 * 1024


def dft_tables():
    order = np.concatenate([np.arange(0, SUB, 2), np.arange(1, SUB, 2)])
    angles = 2.0 * np.pi * np.arange(SUB)[:, None] * (order[None, :] + 0.5) / (2 * SUB)
    forward = np.concatenate([np.cos(angles), -np.sin(angles)], axis=1)
    pair = []
    for table in (forward, forward.T / SUB):
        high = table.astype(jnp.bfloat16)
        low = (table - high.astype(np.float64)).astype(jnp.bfloat16)
        pair.append(jnp.asarray(np.stack([high, low])))
    return pair


def dot(left, right):
    return jnp.dot(left, right, preferred_element_type=F32)


def two_terms(values):
    high = values.astype(BF16)
    return high, (values - high.astype(F32)).astype(BF16)


def dot_terms(values, table):
    high, low = two_terms(values)
    return dot(high, table[0]) + dot(high, table[1]) + dot(low, table[0])


def pack_kernel(groups, taps, *refs):
    sources, (pay_ref, decay_ref, rows, frows), held, sems = refs[:5], refs[5:9], refs[9:14], refs[14]
    copies = [pltpu.make_async_copy(src, dst, sems.at[i]) for i, (src, dst) in enumerate(zip(sources, held))]
    for copy in copies:
        copy.start()
    feat_ref, proj_ref, rate_ref, cot_ref, in_ref = held
    channels, block_len = cot_ref.shape
    for copy in copies[:3]:
        copy.wait()
    per = channels // groups
    subs = block_len // SUB
    span = per * subs
    tap_rows = feat_ref.shape[1]
    first = lax.axis_index("ctx") * tap_rows
    positions = (first + lax.broadcasted_iota(jnp.int32, (1, tap_rows), 1)).astype(F32)
    diagonal = lax.broadcasted_iota(jnp.int32, (channels, channels), 0) == lax.broadcasted_iota(
        jnp.int32, (channels, channels), 1
    )
    rates = jnp.sum(jnp.where(diagonal, rate_ref[...], 0.0), axis=1, keepdims=True)
    decay = jnp.exp(-rates * (positions / taps))
    decay_ref[...] = decay
    product = lax.dot_general(
        proj_ref[...],
        feat_ref[...],
        (((0,), (0,)), ((), ())),
        precision=lax.Precision.HIGHEST,
        preferred_element_type=F32,
    )
    high, low = two_terms(decay * product)
    high = high.astype(F32)
    low = low.astype(F32)
    for group in range(groups):
        own = slice(group * per, (group + 1) * per)
        for half in range(2):
            lanes = slice(half * LANES, (half + 1) * LANES)
            base = half * 2 * per
            frows[group, base : base + per, :] = high[own, lanes]
            frows[group, base + per : base + 2 * per, :] = low[own, lanes]
    pay_ref[:, 4 * span :, :] = frows[...].astype(BF16)
    for which, ref in enumerate((cot_ref, in_ref)):
        copies[3 + which].wait()
        for sub in range(subs):
            for half in range(2):
                start = sub * SUB + half * LANES
                rows[2 * which + half, pl.ds(sub, channels, stride=subs), :] = ref[:, start : start + LANES].astype(F32)
    for part in range(4):
        for group in range(groups):
            pay_ref[group, part * span : (part + 1) * span, :] = rows[part, group * span : (group + 1) * span, :].astype(BF16)


def block_spectra(recv_ref, base, table_ref, store):
    groups = recv_ref.shape[0]
    span = 32
    per, subs = 4, 8
    step = 4
    for first in range(0, groups, step):
        halves = [
            recv_ref[first : first + step, base + half * span : base + (half + 1) * span, :].reshape(step * span, LANES)
            for half in range(2)
        ]
        left = jnp.concatenate(halves, axis=1)
        result = dot(left, table_ref[0]) + dot(left, table_ref[1])
        for src in range(step):
            for chan in range(per):
                row = (src * per + chan) * subs
                for tile in range(4):
                    store(chan, tile, (first + src) * subs, result[row : row + subs, tile * LANES : (tile + 1) * LANES])


def taps_kernel(recv_ref, fwd_ref, inv_ref, win_ref, grad_ref, cot_spec, in_spec, sums, spec):
    groups = recv_ref.shape[0]
    per, subs, lags = 4, 8, 16
    blocks = groups * subs

    def store_cot(chan, tile, row, value):
        cot_spec[chan, tile, row : row + subs, :] = value

    def store_in(chan, tile, row, value):
        in_spec[chan, tile, row : row + subs, :] = value

    block_spectra(recv_ref, 0, fwd_ref, store_cot)
    cot_spec[:, :, blocks:, :] = jnp.zeros((per, 4, subs, LANES), F32)
    block_spectra(recv_ref, 64, fwd_ref, store_in)
    win_ref[:, :, blocks:, :] = jnp.zeros((per, 4, lags, LANES), F32)
    for chan in range(per):
        now = [cot_spec[chan, tile, 0:blocks, :] for tile in range(4)]
        nxt = [cot_spec[chan, tile, 1 : blocks + 1, :] for tile in range(4)]
        win_ref[chan, 0, 0:blocks, :] = now[0] + nxt[2]
        win_ref[chan, 1, 0:blocks, :] = now[1] - nxt[3]
        win_ref[chan, 2, 0:blocks, :] = now[2] - nxt[0]
        win_ref[chan, 3, 0:blocks, :] = now[3] + nxt[1]

    def one(index, carry):
        chan = index // 2
        half = index % 2
        acc_re = [None] * lags
        acc_im = [None] * lags
        for src in range(groups):
            left_re = in_spec[chan, half, src * subs : (src + 1) * subs, :]
            left_im = in_spec[chan, 2 + half, src * subs : (src + 1) * subs, :]
            for lag in range(lags):
                row = src * subs + lag
                win_re = win_ref[chan, half, row : row + subs, :]
                win_im = win_ref[chan, 2 + half, row : row + subs, :]
                term_re = left_re * win_re + left_im * win_im
                term_im = left_re * win_im - left_im * win_re
                acc_re[lag] = term_re if src == 0 else acc_re[lag] + term_re
                acc_im[lag] = term_im if src == 0 else acc_im[lag] + term_im
        for part, acc in enumerate((acc_re, acc_im)):
            for lag in range(lags):
                sums[part, lag * subs : (lag + 1) * subs, :] = acc[lag]
            total = sums[part, pl.ds(0, lags, stride=subs), :]
            for sub in range(1, subs):
                total = total + sums[part, pl.ds(sub, lags, stride=subs), :]
            spec[2 * part + half, pl.ds(chan, lags, stride=per), :] = total
        return carry

    lax.fori_loop(0, 2 * per, one, 0)
    left = jnp.concatenate([spec[tile] for tile in range(4)], axis=1)
    result = dot_terms(left, inv_ref)
    for lag in range(lags):
        own = slice(lag * per, (lag + 1) * per)
        grad_ref[lag, 0:per, :] = result[own, 0:LANES]
        grad_ref[lag, per : 2 * per, :] = result[own, LANES:]


def inputs_kernel(recv_ref, win_ref, fwd_ref, inv_ref, grad_ref, frows, fspec, spec):
    groups = recv_ref.shape[0]
    per, subs, lags = 4, 8, 16
    blocks = groups * subs
    frows[...] = recv_ref[:, 128:144, :].astype(F32).reshape(groups * 16, LANES)
    terms = []
    for term in range(2):
        chans = []
        for chan in range(per):
            halves = [frows[pl.ds(half * 2 * per + term * per + chan, lags, stride=16), :] for half in range(2)]
            chans.append(jnp.concatenate(halves, axis=1))
        terms.append(jnp.concatenate(chans, axis=0).astype(BF16))
    result = dot(terms[0], fwd_ref[0]) + dot(terms[0], fwd_ref[1]) + dot(terms[1], fwd_ref[0])
    for tile in range(4):
        for chan in range(per):
            fspec[chan, tile] = result[chan * lags : (chan + 1) * lags, tile * LANES : (tile + 1) * LANES]

    def one(index, carry):
        chan = index // 2
        half = index % 2
        filt_re = [jnp.broadcast_to(fspec[chan, half, lag : lag + 1, :], (subs, LANES)) for lag in range(lags)]
        filt_im = [jnp.broadcast_to(fspec[chan, 2 + half, lag : lag + 1, :], (subs, LANES)) for lag in range(lags)]
        for src in range(groups):
            acc_re = None
            acc_im = None
            for lag in range(lags):
                row = src * subs + lag
                win_re = win_ref[chan, half, row : row + subs, :]
                win_im = win_ref[chan, 2 + half, row : row + subs, :]
                term_re = filt_re[lag] * win_re + filt_im[lag] * win_im
                term_im = filt_re[lag] * win_im - filt_im[lag] * win_re
                acc_re = term_re if lag == 0 else acc_re + term_re
                acc_im = term_im if lag == 0 else acc_im + term_im
            spec[chan, half, src * subs : (src + 1) * subs, :] = acc_re
            spec[chan, 2 + half, src * subs : (src + 1) * subs, :] = acc_im
        return carry

    lax.fori_loop(0, 2 * per, one, 0)
    for first in range(0, per, 2):
        pair = []
        for chan in (first, first + 1):
            left = jnp.concatenate([spec[chan, tile] for tile in range(4)], axis=1)
            pair.append(dot_terms(left, inv_ref).reshape(groups, subs, SUB))
        both = jnp.concatenate(pair, axis=1)
        grad_ref[:, first * subs : (first + 2) * subs, :] = both.astype(BF16)


def features_kernel(grad_ref, decay_ref, proj_ref, out_ref, part_ref):
    groups = grad_ref.shape[0]
    per = grad_ref.shape[1] // 2
    for group in range(groups):
        own = slice(group * per, (group + 1) * per)
        out_ref[own, 0:LANES] = grad_ref[group, 0:per, :]
        out_ref[own, LANES:] = grad_ref[group, per : 2 * per, :]
    part_ref[...] = jnp.dot(
        proj_ref[...],
        decay_ref[...] * out_ref[...],
        precision=lax.Precision.HIGHEST,
        preferred_element_type=F32,
    )


def call(kernel, out, scratch, flops, fetched=(), limit=VMEM_LIMIT):
    scratch_shapes = [pltpu.VMEM(shape, F32) for shape in scratch]
    specs = {}
    if fetched:
        scratch_shapes += [pltpu.VMEM(value.shape, value.dtype) for value in fetched]
        scratch_shapes.append(pltpu.SemaphoreType.DMA((len(fetched),)))
        specs["in_specs"] = [pl.BlockSpec(memory_space=pltpu.HBM)] * len(fetched)
    return pl.pallas_call(
        kernel,
        out_shape=out,
        scratch_shapes=scratch_shapes,
        **specs,
        compiler_params=pltpu.CompilerParams(vmem_limit_bytes=limit),
        cost_estimate=pl.CostEstimate(flops=flops, bytes_accessed=1 << 20, transcendentals=0),
    )


def shifted(values, axis, distance, ring):
    size = lax.axis_size(axis)
    route = [(i, i - i % ring + (i + distance) % ring) for i in range(size)]
    return lax.ppermute(values, axis, route)


def summed(values, axis, other):
    size = lax.axis_size(axis)
    half = size // 2
    values = values + lax.ppermute(values, axis, [(i, (i + half) % size) for i in range(size)])
    below = shifted(values, axis, 1, half)
    above = shifted(values, axis, -1, half)
    two = values + above
    three = two + below
    far = (shifted(three, axis, -3, half), shifted(two, axis, 3, half))
    far, other = lax.optimization_barrier((far, other))
    return three + far[0] + far[1], other


def shards(inputs, cotangent, features, projection, decay_rates):
    channels, block_len = inputs.shape
    tap_rows = features.shape[1]
    groups = lax.axis_size("ctx")
    per = channels // groups
    subs = block_len // SUB
    taps = 2 * block_len
    lags = taps // SUB
    shape = jax.ShapeDtypeStruct
    forward, backward = dft_tables()

    def exchanged(values):
        return lax.all_to_all(values, "ctx", 0, 0, tiled=True)

    payload, decay = call(
        lambda *refs: pack_kernel(groups, taps, *refs),
        (shape((groups, 144, LANES), BF16), shape((channels, tap_rows), F32)),
        [(4, channels * subs, LANES), (groups, 16, LANES)],
        1 << 22,
        (features, projection, decay_rates.reshape(1, channels), cotangent, inputs),
        60 * 1024 * 1024,
    )(features, projection, decay_rates.reshape(1, channels), cotangent, inputs)
    received = exchanged(payload)
    blocks = groups * subs
    windows, tap_grads = call(
        taps_kernel,
        (shape((per, 4, blocks + lags, LANES), F32), shape((groups, 2 * per, LANES), F32)),
        [(per, 4, blocks + subs, LANES), (per, 4, blocks, LANES), (2, lags * subs, LANES), (4, per * lags, LANES)],
        1 << 32,
    )(received, forward, backward)
    tap_grads = exchanged(tap_grads)
    x_parts = call(
        inputs_kernel,
        shape((groups, per * subs, SUB), BF16),
        [(groups * 16, LANES), (per, 4, lags, LANES), (per, 4, blocks, LANES)],
        1 << 32,
    )(received, windows, forward, backward)
    tap_grads, x_parts = lax.optimization_barrier((tap_grads, x_parts))
    filter_grad, part = call(
        features_kernel,
        (shape((channels, tap_rows), F32), shape((projection.shape[0], tap_rows), F32)),
        [],
        1 << 22,
    )(tap_grads, decay, projection)
    part, x_parts = lax.optimization_barrier((part, x_parts))
    feature_grad, x_grad = summed(part, "ch", exchanged(x_parts).reshape(channels, block_len))
    return (x_grad, filter_grad, feature_grad)


def solution(mesh):
    placed = (P("ch", "ctx"), P("ch", "ctx"), P(None, "ctx"), P(None, "ch"), P("ch"))
    return jax.shard_map(
        shards,
        mesh=mesh,
        in_specs=placed,
        out_specs=(P("ch", "ctx"), P("ch", "ctx"), P(None, "ctx")),
        check_vma=False,
    )
```

```python
import math

import jax
import jax.numpy as jnp
import numpy as np
from jax import lax
from jax.experimental import pallas as pl
from jax.experimental.pallas import tpu as pltpu
from jax.sharding import Mesh
from jax.sharding import PartitionSpec as P

SUB = 256
LANES = 128
F32 = jnp.float32
BF16 = jnp.bfloat16
VMEM_LIMIT = 40 * 1024 * 1024


def dft_tables():
    order = np.concatenate([np.arange(0, SUB, 2), np.arange(1, SUB, 2)])
    angles = 2.0 * np.pi * np.arange(SUB)[:, None] * (order[None, :] + 0.5) / (2 * SUB)
    forward = np.concatenate([np.cos(angles), -np.sin(angles)], axis=1)
    pair = []
    for table in (forward, forward.T / SUB):
        high = table.astype(jnp.bfloat16)
        low = (table - high.astype(np.float64)).astype(jnp.bfloat16)
        pair.append(jnp.asarray(np.stack([high, low])))
    return pair


def dot(left, right):
    return jnp.dot(left, right, preferred_element_type=F32)


def two_terms(values):
    high = values.astype(BF16)
    return high, (values - high.astype(F32)).astype(BF16)


def dot_terms(values, table):
    high, low = two_terms(values)
    return dot(high, table[0]) + dot(high, table[1]) + dot(low, table[0])


def decay_of(rates, tap_rows, taps):
    channels = rates.shape[1]
    first = lax.axis_index("ctx") * tap_rows
    positions = (first + lax.broadcasted_iota(jnp.int32, (1, tap_rows), 1)).astype(F32)
    across = lax.broadcasted_iota(jnp.int32, (channels, channels), 1)
    diagonal = lax.broadcasted_iota(jnp.int32, (channels, channels), 0) == across
    column = jnp.sum(jnp.where(diagonal, rates, 0.0), axis=1, keepdims=True)
    return jnp.exp(-column * (positions / taps))


def pack_kernel(groups, taps, *refs):
    sources, (pay_ref, both_ref, rows, frows), held, sems = refs[:5], refs[5:9], refs[9:14], refs[14]
    copies = [pltpu.make_async_copy(src, dst, sems.at[i]) for i, (src, dst) in enumerate(zip(sources, held))]
    for copy in copies:
        copy.start()
    feat_ref, proj_ref, rate_ref, cot_ref, in_ref = held
    channels, block_len = cot_ref.shape
    for copy in copies[:3]:
        copy.wait()
    per = channels // groups
    subs = block_len // SUB
    span = per * subs
    decay = decay_of(rate_ref[...], feat_ref.shape[1], taps)
    order = proj_ref.shape[0]
    both_ref[0:order, :] = proj_ref[...]
    both_ref[order:, :] = jnp.broadcast_to(rate_ref[...], (8, channels))
    product = lax.dot_general(
        proj_ref[...],
        feat_ref[...],
        (((0,), (0,)), ((), ())),
        precision=lax.Precision.HIGHEST,
        preferred_element_type=F32,
    )
    high, low = two_terms(decay * product)
    high = high.astype(F32)
    low = low.astype(F32)
    for group in range(groups):
        own = slice(group * per, (group + 1) * per)
        for half in range(2):
            lanes = slice(half * LANES, (half + 1) * LANES)
            base = half * 2 * per
            frows[group, base : base + per, :] = high[own, lanes]
            frows[group, base + per : base + 2 * per, :] = low[own, lanes]
    pay_ref[:, 4 * span :, :] = frows[...].astype(BF16)
    for which, ref in enumerate((cot_ref, in_ref)):
        copies[3 + which].wait()
        for sub in range(subs):
            for half in range(2):
                start = sub * SUB + half * LANES
                rows[2 * which + half, pl.ds(sub, channels, stride=subs), :] = ref[:, start : start + LANES].astype(F32)
    for part in range(4):
        for group in range(groups):
            pay_ref[group, part * span : (part + 1) * span, :] = rows[part, group * span : (group + 1) * span, :].astype(BF16)


def block_spectra(recv_ref, base, table_ref, store):
    groups = recv_ref.shape[0]
    span = 32
    per, subs = 4, 8
    step = 4
    for first in range(0, groups, step):
        halves = [
            recv_ref[first : first + step, base + half * span : base + (half + 1) * span, :].reshape(step * span, LANES)
            for half in range(2)
        ]
        left = jnp.concatenate(halves, axis=1)
        result = dot(left, table_ref[0]) + dot(left, table_ref[1])
        for src in range(step):
            for chan in range(per):
                row = (src * per + chan) * subs
                for tile in range(4):
                    store(chan, tile, (first + src) * subs, result[row : row + subs, tile * LANES : (tile + 1) * LANES])


def taps_kernel(recv_ref, fwd_ref, inv_ref, win_ref, grad_ref, cot_spec, in_spec, sums, spec):
    groups = recv_ref.shape[0]
    per, subs, lags = 4, 8, 16
    blocks = groups * subs

    def store_cot(chan, tile, row, value):
        cot_spec[chan, tile, row : row + subs, :] = value

    def store_in(chan, tile, row, value):
        in_spec[chan, tile, row : row + subs, :] = value

    block_spectra(recv_ref, 0, fwd_ref, store_cot)
    cot_spec[:, :, blocks:, :] = jnp.zeros((per, 4, subs, LANES), F32)
    block_spectra(recv_ref, 64, fwd_ref, store_in)
    win_ref[:, :, blocks:, :] = jnp.zeros((per, 4, lags, LANES), F32)
    for chan in range(per):
        now = [cot_spec[chan, tile, 0:blocks, :] for tile in range(4)]
        nxt = [cot_spec[chan, tile, 1 : blocks + 1, :] for tile in range(4)]
        win_ref[chan, 0, 0:blocks, :] = now[0] + nxt[2]
        win_ref[chan, 1, 0:blocks, :] = now[1] - nxt[3]
        win_ref[chan, 2, 0:blocks, :] = now[2] - nxt[0]
        win_ref[chan, 3, 0:blocks, :] = now[3] + nxt[1]

    def one(index, carry):
        chan = index // 2
        half = index % 2
        acc_re = [None] * lags
        acc_im = [None] * lags
        for src in range(groups):
            left_re = in_spec[chan, half, src * subs : (src + 1) * subs, :]
            left_im = in_spec[chan, 2 + half, src * subs : (src + 1) * subs, :]
            for lag in range(lags):
                row = src * subs + lag
                win_re = win_ref[chan, half, row : row + subs, :]
                win_im = win_ref[chan, 2 + half, row : row + subs, :]
                term_re = left_re * win_re + left_im * win_im
                term_im = left_re * win_im - left_im * win_re
                acc_re[lag] = term_re if src == 0 else acc_re[lag] + term_re
                acc_im[lag] = term_im if src == 0 else acc_im[lag] + term_im
        for part, acc in enumerate((acc_re, acc_im)):
            for lag in range(lags):
                sums[part, lag * subs : (lag + 1) * subs, :] = acc[lag]
            total = sums[part, pl.ds(0, lags, stride=subs), :]
            for sub in range(1, subs):
                total = total + sums[part, pl.ds(sub, lags, stride=subs), :]
            spec[2 * part + half, pl.ds(chan, lags, stride=per), :] = total
        return carry

    lax.fori_loop(0, 2 * per, one, 0)
    left = jnp.concatenate([spec[tile] for tile in range(4)], axis=1)
    result = dot_terms(left, inv_ref)
    for lag in range(lags):
        own = slice(lag * per, (lag + 1) * per)
        for copy in range(2):
            grad_ref[2 * lag + copy, 0:per, :] = result[own, 0:LANES]
            grad_ref[2 * lag + copy, per : 2 * per, :] = result[own, LANES:]


def inputs_kernel(recv_ref, win_ref, fwd_ref, inv_ref, grad_ref, frows, fspec, spec):
    groups = recv_ref.shape[0]
    per, subs, lags = 4, 8, 16
    blocks = groups * subs
    frows[...] = recv_ref[:, 128:144, :].astype(F32).reshape(groups * 16, LANES)
    terms = []
    for term in range(2):
        chans = []
        for chan in range(per):
            halves = [frows[pl.ds(half * 2 * per + term * per + chan, lags, stride=16), :] for half in range(2)]
            chans.append(jnp.concatenate(halves, axis=1))
        terms.append(jnp.concatenate(chans, axis=0).astype(BF16))
    result = dot(terms[0], fwd_ref[0]) + dot(terms[0], fwd_ref[1]) + dot(terms[1], fwd_ref[0])
    for tile in range(4):
        for chan in range(per):
            fspec[chan, tile] = result[chan * lags : (chan + 1) * lags, tile * LANES : (tile + 1) * LANES]

    def one(index, carry):
        chan = index // 2
        half = index % 2
        filt_re = [jnp.broadcast_to(fspec[chan, half, lag : lag + 1, :], (subs, LANES)) for lag in range(lags)]
        filt_im = [jnp.broadcast_to(fspec[chan, 2 + half, lag : lag + 1, :], (subs, LANES)) for lag in range(lags)]
        for src in range(groups):
            acc_re = None
            acc_im = None
            for lag in range(lags):
                row = src * subs + lag
                win_re = win_ref[chan, half, row : row + subs, :]
                win_im = win_ref[chan, 2 + half, row : row + subs, :]
                term_re = filt_re[lag] * win_re + filt_im[lag] * win_im
                term_im = filt_re[lag] * win_im - filt_im[lag] * win_re
                acc_re = term_re if lag == 0 else acc_re + term_re
                acc_im = term_im if lag == 0 else acc_im + term_im
            spec[chan, half, src * subs : (src + 1) * subs, :] = acc_re
            spec[chan, 2 + half, src * subs : (src + 1) * subs, :] = acc_im
        return carry

    lax.fori_loop(0, 2 * per, one, 0)
    for first in range(0, per, 2):
        pair = []
        for chan in (first, first + 1):
            left = jnp.concatenate([spec[chan, tile] for tile in range(4)], axis=1)
            pair.append(dot_terms(left, inv_ref).reshape(groups, subs, SUB))
        both = jnp.concatenate(pair, axis=1)
        grad_ref[:, first * subs : (first + 2) * subs, :] = both.astype(BF16)


def features_kernel(taps, grad_ref, mine_ref, other_ref, out_ref, part_ref, held):
    groups = grad_ref.shape[0] // 2
    per = grad_ref.shape[1] // 2
    channels, tap_rows = out_ref.shape
    order = mine_ref.shape[0] - 8
    me = lax.axis_index("x_hi")
    for group in range(groups):
        own = slice(group * per, (group + 1) * per)
        for ref, source in ((out_ref, 2 * group + me), (held, 2 * group + 1 - me)):
            ref[own, 0:LANES] = grad_ref[source, 0:per, :]
            ref[own, LANES:] = grad_ref[source, per : 2 * per, :]
    total = None
    for both, grads in ((mine_ref, out_ref), (other_ref, held)):
        decay = decay_of(both[order : order + 1, :], tap_rows, taps)
        left_high, left_low = two_terms(both[0:order, :])
        high, low = two_terms(decay * grads[...])
        term = dot(left_high, high) + dot(left_high, low) + dot(left_low, high)
        total = term if total is None else total + term
    part_ref[...] = total


def call(kernel, out, scratch, flops, fetched=(), limit=VMEM_LIMIT):
    scratch_shapes = [pltpu.VMEM(shape, F32) for shape in scratch]
    specs = {}
    if fetched:
        scratch_shapes += [pltpu.VMEM(value.shape, value.dtype) for value in fetched]
        scratch_shapes.append(pltpu.SemaphoreType.DMA((len(fetched),)))
        specs["in_specs"] = [pl.BlockSpec(memory_space=pltpu.HBM)] * len(fetched)
    return pl.pallas_call(
        kernel,
        out_shape=out,
        scratch_shapes=scratch_shapes,
        **specs,
        compiler_params=pltpu.CompilerParams(vmem_limit_bytes=limit),
        cost_estimate=pl.CostEstimate(flops=flops, bytes_accessed=1 << 20, transcendentals=0),
    )


def shifted(values, axis, distance):
    size = lax.axis_size(axis)
    return lax.ppermute(values, axis, [(i, (i + distance) % size) for i in range(size)])


def summed(values, axis, beside):
    below = shifted(values, axis, 1)
    above = shifted(values, axis, -1)
    two = values + above
    three = two + below
    far = (shifted(three, axis, -3), shifted(two, axis, 3))
    far, beside = lax.optimization_barrier((far, beside))
    return three + far[0] + far[1], beside


def shards(inputs, cotangent, features, projection, decay_rates):
    channels, block_len = inputs.shape
    tap_rows = features.shape[1]
    groups = lax.axis_size("ctx")
    per = channels // groups
    subs = block_len // SUB
    taps = 2 * block_len
    lags = taps // SUB
    shape = jax.ShapeDtypeStruct
    forward, backward = dft_tables()

    def exchanged(values, axes):
        return lax.all_to_all(values, axes, 0, 0, tiled=True)

    order = projection.shape[0]
    payload, both = call(
        lambda *refs: pack_kernel(groups, taps, *refs),
        (shape((groups, 144, LANES), BF16), shape((order + 8, channels), F32)),
        [(4, channels * subs, LANES), (groups, 16, LANES)],
        1 << 22,
        (features, projection, decay_rates.reshape(1, channels), cotangent, inputs),
        60 * 1024 * 1024,
    )(features, projection, decay_rates.reshape(1, channels), cotangent, inputs)
    other = lax.ppermute(both, "x_hi", [(0, 1), (1, 0)])
    received, other = lax.optimization_barrier((exchanged(payload, "ctx"), other))
    blocks = groups * subs
    windows, tap_grads = call(
        taps_kernel,
        (shape((per, 4, blocks + lags, LANES), F32), shape((2 * groups, 2 * per, LANES), F32)),
        [(per, 4, blocks + subs, LANES), (per, 4, blocks, LANES), (2, lags * subs, LANES), (4, per * lags, LANES)],
        1 << 32,
    )(received, forward, backward)
    tap_grads = exchanged(tap_grads, ("ctx", "x_hi"))
    x_parts = call(
        inputs_kernel,
        shape((groups, per * subs, SUB), BF16),
        [(groups * 16, LANES), (per, 4, lags, LANES), (per, 4, blocks, LANES)],
        1 << 32,
    )(received, windows, forward, backward)
    tap_grads, x_parts = lax.optimization_barrier((tap_grads, x_parts))
    filter_grad, part = call(
        lambda *refs: features_kernel(taps, *refs),
        (shape((channels, tap_rows), F32), shape((order, tap_rows), F32)),
        [(channels, tap_rows)],
        1 << 22,
    )(tap_grads, both, other)
    part, x_parts = lax.optimization_barrier((part, x_parts))
    x_grad = exchanged(x_parts, "ctx").reshape(channels, block_len)
    feature_grad, x_grad = summed(part, "z", x_grad)
    return (x_grad, filter_grad, feature_grad)


def solution(mesh):
    whole = mesh.shape["ch"]
    mesh = Mesh(mesh.devices.reshape(mesh.shape["ctx"], 2, whole // 2), ("ctx", "x_hi", "z"))
    split = ("x_hi", "z")
    placed = (P(split, "ctx"), P(split, "ctx"), P(None, "ctx"), P(None, split), P(split))
    return jax.shard_map(
        shards,
        mesh=mesh,
        in_specs=placed,
        out_specs=(P(split, "ctx"), P(split, "ctx"), P(None, "ctx")),
        check_vma=False,
    )
```

```python
import math

import jax
import jax.numpy as jnp
import numpy as np
from jax import lax
from jax.experimental import pallas as pl
from jax.experimental.pallas import tpu as pltpu
from jax.sharding import Mesh
from jax.sharding import PartitionSpec as P

SUB = 256
LANES = 128
F32 = jnp.float32
BF16 = jnp.bfloat16
VMEM_LIMIT = 40 * 1024 * 1024


def dft_tables():
    order = np.concatenate([np.arange(0, SUB, 2), np.arange(1, SUB, 2)])
    angles = 2.0 * np.pi * np.arange(SUB)[:, None] * (order[None, :] + 0.5) / (2 * SUB)
    forward = np.concatenate([np.cos(angles), -np.sin(angles)], axis=1)
    pair = []
    for table in (forward, forward.T / SUB):
        high = table.astype(jnp.bfloat16)
        low = (table - high.astype(np.float64)).astype(jnp.bfloat16)
        pair.append(jnp.asarray(np.stack([high, low])))
    return pair


def dot(left, right):
    return jnp.dot(left, right, preferred_element_type=F32)


def two_terms(values):
    high = values.astype(BF16)
    return high, (values - high.astype(F32)).astype(BF16)


def dot_terms(values, table):
    high, low = two_terms(values)
    return dot(high, table[0]) + dot(high, table[1]) + dot(low, table[0])


def decay_of(rates, tap_rows, taps):
    channels = rates.shape[1]
    first = lax.axis_index("ctx") * tap_rows
    positions = (first + lax.broadcasted_iota(jnp.int32, (1, tap_rows), 1)).astype(F32)
    across = lax.broadcasted_iota(jnp.int32, (channels, channels), 1)
    diagonal = lax.broadcasted_iota(jnp.int32, (channels, channels), 0) == across
    column = jnp.sum(jnp.where(diagonal, rates, 0.0), axis=1, keepdims=True)
    return jnp.exp(-column * (positions / taps))


def pack_kernel(groups, taps, *refs):
    sources, (pay_ref, both_ref, rows, frows), held, sems = refs[:5], refs[5:9], refs[9:14], refs[14]
    copies = [pltpu.make_async_copy(src, dst, sems.at[i]) for i, (src, dst) in enumerate(zip(sources, held))]
    for copy in copies:
        copy.start()
    feat_ref, proj_ref, rate_ref, cot_ref, in_ref = held
    channels, block_len = cot_ref.shape
    for copy in copies[:3]:
        copy.wait()
    per = channels // groups
    subs = block_len // SUB
    span = per * subs
    decay = decay_of(rate_ref[...], feat_ref.shape[1], taps)
    order = proj_ref.shape[0]
    both_ref[0:order, :] = proj_ref[...]
    both_ref[order:, :] = jnp.broadcast_to(rate_ref[...], (8, channels))
    product = lax.dot_general(
        proj_ref[...],
        feat_ref[...],
        (((0,), (0,)), ((), ())),
        precision=lax.Precision.HIGHEST,
        preferred_element_type=F32,
    )
    high, low = two_terms(decay * product)
    high = high.astype(F32)
    low = low.astype(F32)
    for group in range(groups):
        own = slice(group * per, (group + 1) * per)
        for half in range(2):
            lanes = slice(half * LANES, (half + 1) * LANES)
            base = half * 2 * per
            frows[group, base : base + per, :] = high[own, lanes]
            frows[group, base + per : base + 2 * per, :] = low[own, lanes]
    pay_ref[:, 4 * span :, :] = frows[...].astype(BF16)
    for which, ref in enumerate((cot_ref, in_ref)):
        copies[3 + which].wait()
        for sub in range(subs):
            for half in range(2):
                start = sub * SUB + half * LANES
                rows[2 * which + half, pl.ds(sub, channels, stride=subs), :] = ref[:, start : start + LANES].astype(F32)
    for part in range(4):
        for group in range(groups):
            pay_ref[group, part * span : (part + 1) * span, :] = rows[part, group * span : (group + 1) * span, :].astype(BF16)


def block_spectra(recv_ref, base, table_ref, store):
    groups = recv_ref.shape[0]
    span = 32
    per, subs = 4, 8
    step = 4
    for first in range(0, groups, step):
        halves = [
            recv_ref[first : first + step, base + half * span : base + (half + 1) * span, :].reshape(step * span, LANES)
            for half in range(2)
        ]
        left = jnp.concatenate(halves, axis=1)
        result = dot(left, table_ref[0]) + dot(left, table_ref[1])
        for src in range(step):
            for chan in range(per):
                row = (src * per + chan) * subs
                for tile in range(4):
                    store(chan, tile, (first + src) * subs, result[row : row + subs, tile * LANES : (tile + 1) * LANES])


def taps_kernel(recv_ref, fwd_ref, inv_ref, win_ref, grad_ref, cot_spec, in_spec, sums, spec):
    groups = recv_ref.shape[0]
    per, subs, lags = 4, 8, 16
    blocks = groups * subs

    def store_cot(chan, tile, row, value):
        cot_spec[chan, tile, row : row + subs, :] = value

    def store_in(chan, tile, row, value):
        in_spec[chan, tile, row : row + subs, :] = value

    block_spectra(recv_ref, 0, fwd_ref, store_cot)
    cot_spec[:, :, blocks:, :] = jnp.zeros((per, 4, subs, LANES), F32)
    block_spectra(recv_ref, 64, fwd_ref, store_in)
    win_ref[:, :, blocks:, :] = jnp.zeros((per, 4, lags, LANES), F32)
    for chan in range(per):
        now = [cot_spec[chan, tile, 0:blocks, :] for tile in range(4)]
        nxt = [cot_spec[chan, tile, 1 : blocks + 1, :] for tile in range(4)]
        win_ref[chan, 0, 0:blocks, :] = now[0] + nxt[2]
        win_ref[chan, 1, 0:blocks, :] = now[1] - nxt[3]
        win_ref[chan, 2, 0:blocks, :] = now[2] - nxt[0]
        win_ref[chan, 3, 0:blocks, :] = now[3] + nxt[1]

    def one(index, carry):
        chan = index // 2
        half = index % 2
        acc_re = [None] * lags
        acc_im = [None] * lags
        for src in range(groups):
            left_re = in_spec[chan, half, src * subs : (src + 1) * subs, :]
            left_im = in_spec[chan, 2 + half, src * subs : (src + 1) * subs, :]
            for lag in range(lags):
                row = src * subs + lag
                win_re = win_ref[chan, half, row : row + subs, :]
                win_im = win_ref[chan, 2 + half, row : row + subs, :]
                term_re = left_re * win_re + left_im * win_im
                term_im = left_re * win_im - left_im * win_re
                acc_re[lag] = term_re if src == 0 else acc_re[lag] + term_re
                acc_im[lag] = term_im if src == 0 else acc_im[lag] + term_im
        for part, acc in enumerate((acc_re, acc_im)):
            for lag in range(lags):
                sums[part, lag * subs : (lag + 1) * subs, :] = acc[lag]
            total = sums[part, pl.ds(0, lags, stride=subs), :]
            for sub in range(1, subs):
                total = total + sums[part, pl.ds(sub, lags, stride=subs), :]
            spec[2 * part + half, pl.ds(chan, lags, stride=per), :] = total
        return carry

    lax.fori_loop(0, 2 * per, one, 0)
    left = jnp.concatenate([spec[tile] for tile in range(4)], axis=1)
    result = dot_terms(left, inv_ref)
    for lag in range(lags):
        own = slice(lag * per, (lag + 1) * per)
        for copy in range(2):
            grad_ref[2 * lag + copy, 0:per, :] = result[own, 0:LANES]
            grad_ref[2 * lag + copy, per : 2 * per, :] = result[own, LANES:]


def inputs_kernel(recv_ref, win_ref, fwd_ref, inv_ref, grad_ref, frows, fspec, spec):
    groups = recv_ref.shape[0]
    per, subs, lags = 4, 8, 16
    blocks = groups * subs
    frows[...] = recv_ref[:, 128:144, :].astype(F32).reshape(groups * 16, LANES)
    terms = []
    for term in range(2):
        chans = []
        for chan in range(per):
            halves = [frows[pl.ds(half * 2 * per + term * per + chan, lags, stride=16), :] for half in range(2)]
            chans.append(jnp.concatenate(halves, axis=1))
        terms.append(jnp.concatenate(chans, axis=0).astype(BF16))
    result = dot(terms[0], fwd_ref[0]) + dot(terms[0], fwd_ref[1]) + dot(terms[1], fwd_ref[0])
    for tile in range(4):
        for chan in range(per):
            fspec[chan, tile] = result[chan * lags : (chan + 1) * lags, tile * LANES : (tile + 1) * LANES]

    def one(index, carry):
        chan = index // 2
        half = index % 2
        filt_re = [jnp.broadcast_to(fspec[chan, half, lag : lag + 1, :], (subs, LANES)) for lag in range(lags)]
        filt_im = [jnp.broadcast_to(fspec[chan, 2 + half, lag : lag + 1, :], (subs, LANES)) for lag in range(lags)]
        for src in range(groups):
            acc_re = None
            acc_im = None
            for lag in range(lags):
                row = src * subs + lag
                win_re = win_ref[chan, half, row : row + subs, :]
                win_im = win_ref[chan, 2 + half, row : row + subs, :]
                term_re = filt_re[lag] * win_re + filt_im[lag] * win_im
                term_im = filt_re[lag] * win_im - filt_im[lag] * win_re
                acc_re = term_re if lag == 0 else acc_re + term_re
                acc_im = term_im if lag == 0 else acc_im + term_im
            spec[chan, half, src * subs : (src + 1) * subs, :] = acc_re
            spec[chan, 2 + half, src * subs : (src + 1) * subs, :] = acc_im
        return carry

    lax.fori_loop(0, 2 * per, one, 0)
    for first in range(0, per, 2):
        pair = []
        for chan in (first, first + 1):
            left = jnp.concatenate([spec[chan, tile] for tile in range(4)], axis=1)
            pair.append(dot_terms(left, inv_ref).reshape(groups, subs, SUB))
        both = jnp.concatenate(pair, axis=1)
        grad_ref[:, first * subs : (first + 2) * subs, :] = both.astype(BF16)


def features_kernel(taps, grad_ref, mine_ref, other_ref, out_ref, part_ref, held):
    groups = grad_ref.shape[0] // 2
    per = grad_ref.shape[1] // 2
    channels, tap_rows = out_ref.shape
    order = mine_ref.shape[0] - 8
    me = lax.axis_index("x_hi")
    for group in range(groups):
        own = slice(group * per, (group + 1) * per)
        for ref, source in ((out_ref, 2 * group + me), (held, 2 * group + 1 - me)):
            ref[own, 0:LANES] = grad_ref[source, 0:per, :]
            ref[own, LANES:] = grad_ref[source, per : 2 * per, :]
    total = None
    for both, grads in ((mine_ref, out_ref), (other_ref, held)):
        decay = decay_of(both[order : order + 1, :], tap_rows, taps)
        left_high, left_low = two_terms(both[0:order, :])
        high, low = two_terms(decay * grads[...])
        term = dot(left_high, high) + dot(left_high, low) + dot(left_low, high)
        total = term if total is None else total + term
    part_ref[...] = total


def call(kernel, out, scratch, flops, fetched=(), limit=VMEM_LIMIT):
    scratch_shapes = [pltpu.VMEM(shape, F32) for shape in scratch]
    specs = {}
    if fetched:
        scratch_shapes += [pltpu.VMEM(value.shape, value.dtype) for value in fetched]
        scratch_shapes.append(pltpu.SemaphoreType.DMA((len(fetched),)))
        specs["in_specs"] = [pl.BlockSpec(memory_space=pltpu.HBM)] * len(fetched)
    return pl.pallas_call(
        kernel,
        out_shape=out,
        scratch_shapes=scratch_shapes,
        **specs,
        compiler_params=pltpu.CompilerParams(vmem_limit_bytes=limit),
        cost_estimate=pl.CostEstimate(flops=flops, bytes_accessed=1 << 20, transcendentals=0),
    )


def swapped(values, axis, mask):
    return lax.ppermute(values, axis, [(i, i ^ mask) for i in range(lax.axis_size(axis))])


def paired(values, axis, partner):
    return lax.ppermute(values, axis, list(enumerate(partner)))


FAR = (6, 7, 4, 5, 2, 3, 0, 1)


def summed(values, axis, beside):
    near = [swapped(values, axis, mask) for mask in (1,3,2)]
    values = values + near[0]+near[1]+near[2]
    far = paired(values, axis, FAR)
    far, beside = lax.optimization_barrier((far, beside))
    return values + far, beside


def shards(inputs, cotangent, features, projection, decay_rates):
    channels, block_len = inputs.shape
    tap_rows = features.shape[1]
    groups = lax.axis_size("ctx")
    per = channels // groups
    subs = block_len // SUB
    taps = 2 * block_len
    lags = taps // SUB
    shape = jax.ShapeDtypeStruct
    forward, backward = dft_tables()

    def exchanged(values, axes):
        return lax.all_to_all(values, axes, 0, 0, tiled=True)

    order = projection.shape[0]
    payload, both = call(
        lambda *refs: pack_kernel(groups, taps, *refs),
        (shape((groups, 144, LANES), BF16), shape((order + 8, channels), F32)),
        [(4, channels * subs, LANES), (groups, 16, LANES)],
        1 << 22,
        (features, projection, decay_rates.reshape(1, channels), cotangent, inputs),
        60 * 1024 * 1024,
    )(features, projection, decay_rates.reshape(1, channels), cotangent, inputs)
    other = lax.ppermute(both, "x_hi", [(0, 1), (1, 0)])
    received, other = lax.optimization_barrier((exchanged(payload, "ctx"), other))
    blocks = groups * subs
    windows, tap_grads = call(
        taps_kernel,
        (shape((per, 4, blocks + lags, LANES), F32), shape((2 * groups, 2 * per, LANES), F32)),
        [(per, 4, blocks + subs, LANES), (per, 4, blocks, LANES), (2, lags * subs, LANES), (4, per * lags, LANES)],
        1 << 32,
    )(received, forward, backward)
    tap_grads = exchanged(tap_grads, ("ctx", "x_hi"))
    x_parts = call(
        inputs_kernel,
        shape((groups, per * subs, SUB), BF16),
        [(groups * 16, LANES), (per, 4, lags, LANES), (per, 4, blocks, LANES)],
        1 << 32,
    )(received, windows, forward, backward)
    tap_grads, x_parts = lax.optimization_barrier((tap_grads, x_parts))
    filter_grad, part = call(
        lambda *refs: features_kernel(taps, *refs),
        (shape((channels, tap_rows), F32), shape((order, tap_rows), F32)),
        [(channels, tap_rows)],
        1 << 22,
    )(tap_grads, both, other)
    part, x_parts = lax.optimization_barrier((part, x_parts))
    x_grad = exchanged(x_parts, "ctx").reshape(channels, block_len)
    feature_grad, x_grad = summed(part, "z", x_grad)
    return (x_grad, filter_grad, feature_grad)


def solution(mesh):
    whole = mesh.shape["ch"]
    mesh = Mesh(mesh.devices.reshape(mesh.shape["ctx"], 2, whole // 2), ("ctx", "x_hi", "z"))
    split = ("x_hi", "z")
    placed = (P(split, "ctx"), P(split, "ctx"), P(None, "ctx"), P(None, split), P(split))
    return jax.shard_map(
        shards,
        mesh=mesh,
        in_specs=placed,
        out_specs=(P(split, "ctx"), P(split, "ctx"), P(None, "ctx")),
        check_vma=False,
    )
```

```python
import math

import jax
import jax.numpy as jnp
import numpy as np
from jax import lax
from jax.experimental import pallas as pl
from jax.experimental.pallas import tpu as pltpu
from jax.sharding import Mesh
from jax.sharding import PartitionSpec as P

SUB = 256
LANES = 128
F32 = jnp.float32
BF16 = jnp.bfloat16
VMEM_LIMIT = 40 * 1024 * 1024


def dft_tables():
    order = np.concatenate([np.arange(0, SUB, 2), np.arange(1, SUB, 2)])
    angles = 2.0 * np.pi * np.arange(SUB)[:, None] * (order[None, :] + 0.5) / (2 * SUB)
    forward = np.concatenate([np.cos(angles), -np.sin(angles)], axis=1)
    pair = []
    for table in (forward, forward.T / SUB):
        high = table.astype(jnp.bfloat16)
        low = (table - high.astype(np.float64)).astype(jnp.bfloat16)
        pair.append(jnp.asarray(np.stack([high, low])))
    return pair


def dot(left, right):
    return jnp.dot(left, right, preferred_element_type=F32)


def two_terms(values):
    high = values.astype(BF16)
    return high, (values - high.astype(F32)).astype(BF16)


def dot_terms(values, table):
    high, low = two_terms(values)
    return dot(high, table[0]) + dot(high, table[1]) + dot(low, table[0])


def decay_of(rates, tap_rows, taps):
    channels = rates.shape[1]
    first = lax.axis_index("ctx") * tap_rows
    positions = (first + lax.broadcasted_iota(jnp.int32, (1, tap_rows), 1)).astype(F32)
    across = lax.broadcasted_iota(jnp.int32, (channels, channels), 1)
    diagonal = lax.broadcasted_iota(jnp.int32, (channels, channels), 0) == across
    column = jnp.sum(jnp.where(diagonal, rates, 0.0), axis=1, keepdims=True)
    return jnp.exp(-column * (positions / taps))


def pack_kernel(groups, taps, *refs):
    sources, (pay_ref, both_ref, rows, frows), held, sems = refs[:5], refs[5:9], refs[9:14], refs[14]
    copies = [pltpu.make_async_copy(src, dst, sems.at[i]) for i, (src, dst) in enumerate(zip(sources, held))]
    for copy in copies:
        copy.start()
    feat_ref, proj_ref, rate_ref, cot_ref, in_ref = held
    channels, block_len = cot_ref.shape
    for copy in copies[:3]:
        copy.wait()
    per = channels // groups
    subs = block_len // SUB
    span = per * subs
    decay = decay_of(rate_ref[...], feat_ref.shape[1], taps)
    order = proj_ref.shape[0]
    both_ref[0:order, :] = proj_ref[...]
    both_ref[order:, :] = jnp.broadcast_to(rate_ref[...], (8, channels))
    product = lax.dot_general(
        proj_ref[...],
        feat_ref[...],
        (((0,), (0,)), ((), ())),
        precision=lax.Precision.HIGHEST,
        preferred_element_type=F32,
    )
    high, low = two_terms(decay * product)
    high = high.astype(F32)
    low = low.astype(F32)
    for group in range(groups):
        own = slice(group * per, (group + 1) * per)
        for half in range(2):
            lanes = slice(half * LANES, (half + 1) * LANES)
            base = half * 2 * per
            frows[group, base : base + per, :] = high[own, lanes]
            frows[group, base + per : base + 2 * per, :] = low[own, lanes]
    pay_ref[:, 4 * span :, :] = frows[...].astype(BF16)
    for which, ref in enumerate((cot_ref, in_ref)):
        copies[3 + which].wait()
        for sub in range(subs):
            for half in range(2):
                start = sub * SUB + half * LANES
                rows[2 * which + half, pl.ds(sub, channels, stride=subs), :] = ref[:, start : start + LANES].astype(F32)
    for part in range(4):
        for group in range(groups):
            pay_ref[group, part * span : (part + 1) * span, :] = rows[part, group * span : (group + 1) * span, :].astype(BF16)


def block_spectra(recv_ref, base, table_ref, store):
    groups = recv_ref.shape[0]
    span = 32
    per, subs = 4, 8
    step = 4
    for first in range(0, groups, step):
        halves = [
            recv_ref[first : first + step, base + half * span : base + (half + 1) * span, :].reshape(step * span, LANES)
            for half in range(2)
        ]
        left = jnp.concatenate(halves, axis=1)
        result = dot(left, table_ref[0]) + dot(left, table_ref[1])
        for src in range(step):
            for chan in range(per):
                row = (src * per + chan) * subs
                for tile in range(4):
                    store(chan, tile, (first + src) * subs, result[row : row + subs, tile * LANES : (tile + 1) * LANES])


def products(real, imag):
    return real - imag, real, imag


def window_of(win_ref, mixed, index, which, row, rows):
    if which == 0:
        return win_ref[index, 0, row : row + rows, :]
    return mixed[index, which - 1, row : row + rows, :]


def taps_kernel(recv_ref, fwd_ref, inv_ref, win_ref, grad_ref, cot_spec, in_spec, mixed, sums, spec):
    groups = recv_ref.shape[0]
    per, subs, lags = 4, 8, 16
    blocks = groups * subs

    def store_cot(chan, tile, row, value):
        cot_spec[chan, tile, row : row + subs, :] = value

    def store_in(chan, tile, row, value):
        in_spec[(chan * 2 + tile % 2) * 3 + 1 + tile // 2, row : row + subs, :] = value

    block_spectra(recv_ref, 0, fwd_ref, store_cot)
    cot_spec[:, :, blocks:, :] = jnp.zeros((per, 4, subs, LANES), F32)
    block_spectra(recv_ref, 64, fwd_ref, store_in)
    for ref in (win_ref, mixed):
        ref[:, :, blocks:, :] = jnp.zeros((2 * per, 2, lags, LANES), F32)
    for chan in range(per):
        now = [cot_spec[chan, tile, 0:blocks, :] for tile in range(4)]
        nxt = [cot_spec[chan, tile, 1 : blocks + 1, :] for tile in range(4)]
        parts = ((now[0] + nxt[2], now[2] - nxt[0]), (now[1] - nxt[3], now[3] + nxt[1]))
        for half, (real, imag) in enumerate(parts):
            base = chan * 2 + half
            win_ref[base, 0, 0:blocks, :] = real
            win_ref[base, 1, 0:blocks, :] = imag
            mixed[base, 0, 0:blocks, :] = imag - real
            mixed[base, 1, 0:blocks, :] = real + imag

    for part in range(2 * per):
        in_spec[3 * part] = in_spec[3 * part + 1] - in_spec[3 * part + 2]

    def one(index, carry):
        for which in range(3):
            acc = [None] * lags
            left = None
            for src in range(groups + 1):
                before = left
                if src < groups:
                    left = in_spec[3 * index + which, src * subs : (src + 1) * subs, :]
                for lag in range(subs):
                    row = src * subs + lag
                    window = window_of(win_ref, mixed, index, which, row, subs)
                    if src < groups:
                        acc[lag] = left * window if src == 0 else acc[lag] + left * window
                    if src > 0:
                        far = lag + subs
                        acc[far] = before * window if src == 1 else acc[far] + before * window
            for lag in range(lags):
                sums[3 * index + which, lag * subs : (lag + 1) * subs, :] = acc[lag]
        return carry

    lax.fori_loop(0, 2 * per, one, 0)
    for chan in range(per):
        for half in range(2):
            totals = []
            for which in range(3):
                index = (chan * 2 + half) * 3 + which
                total = sums[index, pl.ds(0, lags, stride=subs), :]
                for sub in range(1, subs):
                    total = total + sums[index, pl.ds(sub, lags, stride=subs), :]
                totals.append(total)
            spec[half, pl.ds(chan, lags, stride=per), :] = totals[0] + totals[2]
            spec[2 + half, pl.ds(chan, lags, stride=per), :] = totals[0] + totals[1]
    left = jnp.concatenate([spec[tile] for tile in range(4)], axis=1)
    result = dot_terms(left, inv_ref)
    for lag in range(lags):
        own = slice(lag * per, (lag + 1) * per)
        for copy in range(2):
            grad_ref[2 * lag + copy, 0:per, :] = result[own, 0:LANES]
            grad_ref[2 * lag + copy, per : 2 * per, :] = result[own, LANES:]


def inputs_kernel(recv_ref, win_ref, fwd_ref, inv_ref, grad_ref, frows, fspec, mixed, spec):
    groups = recv_ref.shape[0]
    per, subs, lags = 4, 8, 16
    frows[...] = recv_ref[:, 128:144, :].astype(F32).reshape(groups * 16, LANES)
    terms = []
    for term in range(2):
        chans = []
        for chan in range(per):
            halves = [frows[pl.ds(half * 2 * per + term * per + chan, lags, stride=16), :] for half in range(2)]
            chans.append(jnp.concatenate(halves, axis=1))
        terms.append(jnp.concatenate(chans, axis=0).astype(BF16))
    result = dot(terms[0], fwd_ref[0]) + dot(terms[0], fwd_ref[1]) + dot(terms[1], fwd_ref[0])
    for chan in range(per):
        rows = result[chan * lags : (chan + 1) * lags]
        for half in range(2):
            real = rows[:, half * LANES : (half + 1) * LANES]
            imag = rows[:, (2 + half) * LANES : (3 + half) * LANES]
            for which, value in enumerate(products(real, imag)):
                fspec[(chan * 2 + half) * 3 + which] = value

    for part in range(2 * per):
        mixed[part, 0] = win_ref[part, 1] - win_ref[part, 0]
        mixed[part, 1] = win_ref[part, 0] + win_ref[part, 1]

    def one(index, carry):
        for which in range(3):
            own = 3 * index + which
            filt = [jnp.broadcast_to(fspec[own, lag : lag + 1, :], (subs, LANES)) for lag in range(lags)]
            low = None
            for src in range(groups + 1):
                before = low
                near = [None, None]
                far = [None, None]
                for lag in range(subs):
                    row = src * subs + lag
                    window = window_of(win_ref, mixed, index, which, row, subs)
                    way = lag % 2
                    if src < groups:
                        term = filt[lag] * window
                        near[way] = term if near[way] is None else near[way] + term
                    if src > 0:
                        term = filt[lag + subs] * window
                        far[way] = term if far[way] is None else far[way] + term
                if src < groups:
                    low = near[0] + near[1]
                if src > 0:
                    spec[own, (src - 1) * subs : src * subs, :] = before + (far[0] + far[1])
        return carry

    lax.fori_loop(0, 2 * per, one, 0)
    for first in range(0, per, 2):
        pair = []
        for chan in (first, first + 1):
            base = chan * 6
            tiles = [spec[base + 3 * half] + spec[base + 3 * half + 2] for half in range(2)]
            tiles += [spec[base + 3 * half] + spec[base + 3 * half + 1] for half in range(2)]
            pair.append(dot_terms(jnp.concatenate(tiles, axis=1), inv_ref).reshape(groups, subs, SUB))
        both = jnp.concatenate(pair, axis=1)
        grad_ref[:, first * subs : (first + 2) * subs, :] = both.astype(BF16)


def features_kernel(taps, grad_ref, mine_ref, other_ref, part_ref, held):
    groups = grad_ref.shape[0] // 2
    per = grad_ref.shape[1] // 2
    tap_rows = part_ref.shape[1]
    order = mine_ref.shape[0] - 8
    me = lax.axis_index("x_hi")
    total = None
    for which, both in enumerate((mine_ref, other_ref)):
        for group in range(groups):
            own = slice(group * per, (group + 1) * per)
            source = 2 * group + (1 - me if which else me)
            held[which, own, 0:LANES] = grad_ref[source, 0:per, :]
            held[which, own, LANES:] = grad_ref[source, per : 2 * per, :]
        decay = decay_of(both[order : order + 1, :], tap_rows, taps)
        left_high, left_low = two_terms(both[0:order, :])
        high, low = two_terms(decay * held[which])
        term = dot(left_high, high) + dot(left_high, low) + dot(left_low, high)
        total = term if total is None else total + term
    part_ref[...] = total


def finish_kernel(recv_ref, grad_ref, near_ref, far_ref, x_ref, filter_ref, feature_ref, rows):
    groups, span = recv_ref.shape[:2]
    per = grad_ref.shape[1] // 2
    channels = x_ref.shape[0]
    subs = x_ref.shape[1] // SUB
    me = lax.axis_index("x_hi")
    feature_ref[...] = near_ref[...] + far_ref[...]
    for group in range(groups):
        own = slice(group * per, (group + 1) * per)
        filter_ref[own, 0:LANES] = grad_ref[2 * group + me, 0:per, :]
        filter_ref[own, LANES:] = grad_ref[2 * group + me, per : 2 * per, :]
        block = recv_ref[group].astype(F32)
        for half in range(2):
            rows[half, group * span : (group + 1) * span, :] = block[:, half * LANES : (half + 1) * LANES]
    for sub in range(subs):
        for half in range(2):
            start = sub * SUB + half * LANES
            x_ref[:, start : start + LANES] = rows[half, pl.ds(sub, channels, stride=subs), :].astype(BF16)


def call(kernel, out, scratch, flops, fetched=(), limit=VMEM_LIMIT):
    scratch_shapes = [pltpu.VMEM(shape, F32) for shape in scratch]
    specs = {}
    if fetched:
        scratch_shapes += [pltpu.VMEM(value.shape, value.dtype) for value in fetched]
        scratch_shapes.append(pltpu.SemaphoreType.DMA((len(fetched),)))
        specs["in_specs"] = [pl.BlockSpec(memory_space=pltpu.HBM)] * len(fetched)
    return pl.pallas_call(
        kernel,
        out_shape=out,
        scratch_shapes=scratch_shapes,
        **specs,
        compiler_params=pltpu.CompilerParams(vmem_limit_bytes=limit),
        cost_estimate=pl.CostEstimate(flops=flops, bytes_accessed=1 << 20, transcendentals=0),
    )


def swapped(values, axis, mask):
    return lax.ppermute(values, axis, [(i, i ^ mask) for i in range(lax.axis_size(axis))])


def paired(values, axis, partner):
    return lax.ppermute(values, axis, list(enumerate(partner)))


FAR = (6, 7, 4, 5, 2, 3, 0, 1)


def halves_of_sum(values, axis):
    near = [swapped(values, axis, mask) for mask in (1, 3, 2)]
    values = values + near[0] + near[1] + near[2]
    return values, paired(values, axis, FAR)


def shards(inputs, cotangent, features, projection, decay_rates):
    channels, block_len = inputs.shape
    tap_rows = features.shape[1]
    groups = lax.axis_size("ctx")
    per = channels // groups
    subs = block_len // SUB
    taps = 2 * block_len
    lags = taps // SUB
    shape = jax.ShapeDtypeStruct
    forward, backward = dft_tables()

    def exchanged(values, axes):
        return lax.all_to_all(values, axes, 0, 0, tiled=True)

    order = projection.shape[0]
    payload, both = call(
        lambda *refs: pack_kernel(groups, taps, *refs),
        (shape((groups, 144, LANES), BF16), shape((order + 8, channels), F32)),
        [(4, channels * subs, LANES), (groups, 16, LANES)],
        1 << 22,
        (features, projection, decay_rates.reshape(1, channels), cotangent, inputs),
        60 * 1024 * 1024,
    )(features, projection, decay_rates.reshape(1, channels), cotangent, inputs)
    other = lax.ppermute(both, "x_hi", [(0, 1), (1, 0)])
    received, other = lax.optimization_barrier((exchanged(payload, "ctx"), other))
    blocks = groups * subs
    mixed = (2 * per, 2, blocks + lags, LANES)
    windows, tap_grads = call(
        taps_kernel,
        (shape((2 * per, 2, blocks + lags, LANES), F32), shape((2 * groups, 2 * per, LANES), F32)),
        [(per, 4, blocks + subs, LANES), (6 * per, blocks, LANES), mixed, (6 * per, lags * subs, LANES), (4, per * lags, LANES)],
        1 << 32,
    )(received, forward, backward)
    tap_grads = exchanged(tap_grads, ("ctx", "x_hi"))
    x_parts = call(
        inputs_kernel,
        shape((groups, per * subs, SUB), BF16),
        [(groups * 16, LANES), (6 * per, lags, LANES), mixed, (6 * per, blocks, LANES)],
        1 << 32,
    )(received, windows, forward, backward)
    tap_grads, x_parts = lax.optimization_barrier((tap_grads, x_parts))
    part = call(
        lambda *refs: features_kernel(taps, *refs),
        shape((order, tap_rows), F32),
        [(2, channels, tap_rows)],
        1 << 22,
    )(tap_grads, both, other)
    part, x_parts = lax.optimization_barrier((part, x_parts))
    near, far = halves_of_sum(part, "z")
    return call(
        finish_kernel,
        (shape((channels, block_len), BF16), shape((channels, tap_rows), F32), shape((order, tap_rows), F32)),
        [(2, channels * subs, LANES)],
        1 << 22,
    )(exchanged(x_parts, "ctx"), tap_grads, near, far)


def solution(mesh):
    whole = mesh.shape["ch"]
    mesh = Mesh(mesh.devices.reshape(mesh.shape["ctx"], 2, whole // 2), ("ctx", "x_hi", "z"))
    split = ("x_hi", "z")
    placed = (P(split, "ctx"), P(split, "ctx"), P(None, "ctx"), P(None, split), P(split))
    return jax.shard_map(
        shards,
        mesh=mesh,
        in_specs=placed,
        out_specs=(P(split, "ctx"), P(split, "ctx"), P(None, "ctx")),
        check_vma=False,
    )
```

```python
import math

import jax
import jax.numpy as jnp
import numpy as np
from jax import lax
from jax.experimental import pallas as pl
from jax.experimental.pallas import tpu as pltpu
from jax.sharding import Mesh
from jax.sharding import PartitionSpec as P

SUB = 256
LANES = 128
F32 = jnp.float32
BF16 = jnp.bfloat16
VMEM_LIMIT = 40 * 1024 * 1024


def dft_tables():
    order = np.concatenate([np.arange(0, SUB, 2), np.arange(1, SUB, 2)])
    angles = 2.0 * np.pi * np.arange(SUB)[:, None] * (order[None, :] + 0.5) / (2 * SUB)
    forward = np.concatenate([np.cos(angles), -np.sin(angles)], axis=1)
    pair = []
    for table in (forward, forward.T / SUB):
        high = table.astype(jnp.bfloat16)
        low = (table - high.astype(np.float64)).astype(jnp.bfloat16)
        pair.append(jnp.asarray(np.stack([high, low])))
    return pair


def dot(left, right):
    return jnp.dot(left, right, preferred_element_type=F32)


def two_terms(values):
    high = values.astype(BF16)
    return high, (values - high.astype(F32)).astype(BF16)


def dot_terms(values, table):
    high, low = two_terms(values)
    return dot(high, table[0]) + dot(high, table[1]) + dot(low, table[0])


def decay_of(rates, tap_rows, taps):
    channels = rates.shape[1]
    first = lax.axis_index("ctx") * tap_rows
    positions = (first + lax.broadcasted_iota(jnp.int32, (1, tap_rows), 1)).astype(F32)
    across = lax.broadcasted_iota(jnp.int32, (channels, channels), 1)
    diagonal = lax.broadcasted_iota(jnp.int32, (channels, channels), 0) == across
    column = jnp.sum(jnp.where(diagonal, rates, 0.0), axis=1, keepdims=True)
    return jnp.exp(-column * (positions / taps))


def pack_kernel(groups, taps, *refs):
    sources, (pay_ref, both_ref, rows, frows), held, sems = refs[:5], refs[5:9], refs[9:14], refs[14]
    copies = [pltpu.make_async_copy(src, dst, sems.at[i]) for i, (src, dst) in enumerate(zip(sources, held))]
    for copy in copies:
        copy.start()
    feat_ref, proj_ref, rate_ref, cot_ref, in_ref = held
    channels, block_len = cot_ref.shape
    for copy in copies[:3]:
        copy.wait()
    per = channels // groups
    subs = block_len // SUB
    span = per * subs
    decay = decay_of(rate_ref[...], feat_ref.shape[1], taps)
    order = proj_ref.shape[0]
    both_ref[0:order, :] = proj_ref[...]
    both_ref[order:, :] = jnp.broadcast_to(rate_ref[...], (8, channels))
    product = lax.dot_general(
        proj_ref[...],
        feat_ref[...],
        (((0,), (0,)), ((), ())),
        precision=lax.Precision.HIGHEST,
        preferred_element_type=F32,
    )
    high, low = two_terms(decay * product)
    high = high.astype(F32)
    low = low.astype(F32)
    for group in range(groups):
        own = slice(group * per, (group + 1) * per)
        for half in range(2):
            lanes = slice(half * LANES, (half + 1) * LANES)
            base = half * 2 * per
            frows[group, base : base + per, :] = high[own, lanes]
            frows[group, base + per : base + 2 * per, :] = low[own, lanes]
    pay_ref[:, 4 * span :, :] = frows[...].astype(BF16)
    for which, ref in enumerate((cot_ref, in_ref)):
        copies[3 + which].wait()
        for sub in range(subs):
            for half in range(2):
                start = sub * SUB + half * LANES
                rows[2 * which + half, pl.ds(sub, channels, stride=subs), :] = ref[:, start : start + LANES].astype(F32)
    for part in range(4):
        for group in range(groups):
            pay_ref[group, part * span : (part + 1) * span, :] = rows[part, group * span : (group + 1) * span, :].astype(BF16)


def block_spectra(recv_ref, base, table_ref, store):
    groups = recv_ref.shape[0]
    span = 32
    per, subs = 4, 8
    step = 4
    for first in range(0, groups, step):
        halves = [
            recv_ref[first : first + step, base + half * span : base + (half + 1) * span, :].reshape(step * span, LANES)
            for half in range(2)
        ]
        left = jnp.concatenate(halves, axis=1)
        result = dot(left, table_ref[0]) + dot(left, table_ref[1])
        for src in range(step):
            for chan in range(per):
                row = (src * per + chan) * subs
                for tile in range(4):
                    store(chan, tile, (first + src) * subs, result[row : row + subs, tile * LANES : (tile + 1) * LANES])


def products(real, imag):
    return real - imag, real, imag


def window_of(win_ref, mixed, index, which, row, rows):
    if which == 0:
        return win_ref[index, 0, row : row + rows, :]
    return mixed[index, which - 1, row : row + rows, :]


def taps_kernel(recv_ref, fwd_ref, inv_ref, win_ref, grad_ref, cot_spec, in_spec, mixed, sums, spec):
    groups = recv_ref.shape[0]
    per, subs, lags = 4, 8, 16
    blocks = groups * subs

    def store_cot(chan, tile, row, value):
        cot_spec[chan, tile, row : row + subs, :] = value

    def store_in(chan, tile, row, value):
        in_spec[(chan * 2 + tile % 2) * 3 + 1 + tile // 2, row : row + subs, :] = value

    block_spectra(recv_ref, 0, fwd_ref, store_cot)
    cot_spec[:, :, blocks:, :] = jnp.zeros((per, 4, subs, LANES), F32)
    block_spectra(recv_ref, 64, fwd_ref, store_in)
    for ref in (win_ref, mixed):
        ref[:, :, blocks:, :] = jnp.zeros((2 * per, 2, lags, LANES), F32)
    for chan in range(per):
        now = [cot_spec[chan, tile, 0:blocks, :] for tile in range(4)]
        nxt = [cot_spec[chan, tile, 1 : blocks + 1, :] for tile in range(4)]
        parts = ((now[0] + nxt[2], now[2] - nxt[0]), (now[1] - nxt[3], now[3] + nxt[1]))
        for half, (real, imag) in enumerate(parts):
            base = chan * 2 + half
            win_ref[base, 0, 0:blocks, :] = real
            win_ref[base, 1, 0:blocks, :] = imag
            mixed[base, 0, 0:blocks, :] = imag - real
            mixed[base, 1, 0:blocks, :] = real + imag

    for part in range(2 * per):
        in_spec[3 * part] = in_spec[3 * part + 1] - in_spec[3 * part + 2]

    def one(index, carry):
        for which in range(3):
            acc = [None] * lags
            left = None
            for src in range(groups + 1):
                before = left
                if src < groups:
                    left = in_spec[3 * index + which, src * subs : (src + 1) * subs, :]
                for lag in range(subs):
                    row = src * subs + lag
                    window = window_of(win_ref, mixed, index, which, row, subs)
                    if src < groups:
                        acc[lag] = left * window if src == 0 else acc[lag] + left * window
                    if src > 0:
                        far = lag + subs
                        acc[far] = before * window if src == 1 else acc[far] + before * window
            for lag in range(lags):
                sums[3 * index + which, lag * subs : (lag + 1) * subs, :] = acc[lag]
        return carry

    lax.fori_loop(0, 2 * per, one, 0)
    for chan in range(per):
        for half in range(2):
            totals = []
            for which in range(3):
                index = (chan * 2 + half) * 3 + which
                total = sums[index, pl.ds(0, lags, stride=subs), :]
                for sub in range(1, subs):
                    total = total + sums[index, pl.ds(sub, lags, stride=subs), :]
                totals.append(total)
            spec[half, pl.ds(chan, lags, stride=per), :] = totals[0] + totals[2]
            spec[2 + half, pl.ds(chan, lags, stride=per), :] = totals[0] + totals[1]
    left = jnp.concatenate([spec[tile] for tile in range(4)], axis=1)
    result = dot_terms(left, inv_ref)
    for lag in range(lags):
        own = slice(lag * per, (lag + 1) * per)
        for copy in range(2):
            grad_ref[2 * lag + copy, 0:per, :] = result[own, 0:LANES]
            grad_ref[2 * lag + copy, per : 2 * per, :] = result[own, LANES:]


def inputs_kernel(recv_ref, win_ref, fwd_ref, inv_ref, grad_ref, frows, fspec, mixed, spec):
    groups = recv_ref.shape[0]
    per, subs, lags = 4, 8, 16
    frows[...] = recv_ref[:, 128:144, :].astype(F32).reshape(groups * 16, LANES)
    terms = []
    for term in range(2):
        chans = []
        for chan in range(per):
            halves = [frows[pl.ds(half * 2 * per + term * per + chan, lags, stride=16), :] for half in range(2)]
            chans.append(jnp.concatenate(halves, axis=1))
        terms.append(jnp.concatenate(chans, axis=0).astype(BF16))
    result = dot(terms[0], fwd_ref[0]) + dot(terms[0], fwd_ref[1]) + dot(terms[1], fwd_ref[0])
    for chan in range(per):
        rows = result[chan * lags : (chan + 1) * lags]
        for half in range(2):
            real = rows[:, half * LANES : (half + 1) * LANES]
            imag = rows[:, (2 + half) * LANES : (3 + half) * LANES]
            for which, value in enumerate(products(real, imag)):
                fspec[(chan * 2 + half) * 3 + which] = value

    for part in range(2 * per):
        mixed[part, 0] = win_ref[part, 1] - win_ref[part, 0]
        mixed[part, 1] = win_ref[part, 0] + win_ref[part, 1]

    def one(index, carry):
        for which in range(3):
            own = 3 * index + which
            filt = [jnp.broadcast_to(fspec[own, lag : lag + 1, :], (subs, LANES)) for lag in range(lags)]
            low = None
            for src in range(groups + 1):
                before = low
                near = [None, None]
                far = [None, None]
                for lag in range(subs):
                    row = src * subs + lag
                    window = window_of(win_ref, mixed, index, which, row, subs)
                    way = lag % 2
                    if src < groups:
                        term = filt[lag] * window
                        near[way] = term if near[way] is None else near[way] + term
                    if src > 0:
                        term = filt[lag + subs] * window
                        far[way] = term if far[way] is None else far[way] + term
                if src < groups:
                    low = near[0] + near[1]
                if src > 0:
                    spec[own, (src - 1) * subs : src * subs, :] = before + (far[0] + far[1])
        return carry

    lax.fori_loop(0, 2 * per, one, 0)
    for first in range(0, per, 2):
        pair = []
        for chan in (first, first + 1):
            base = chan * 6
            tiles = [spec[base + 3 * half] + spec[base + 3 * half + 2] for half in range(2)]
            tiles += [spec[base + 3 * half] + spec[base + 3 * half + 1] for half in range(2)]
            pair.append(dot_terms(jnp.concatenate(tiles, axis=1), inv_ref).reshape(groups, subs, SUB))
        both = jnp.concatenate(pair, axis=1)
        grad_ref[:, first * subs : (first + 2) * subs, :] = both.astype(BF16)


def features_kernel(taps, grad_ref, mine_ref, other_ref, part_ref, held):
    groups = grad_ref.shape[0] // 2
    per = grad_ref.shape[1] // 2
    tap_rows = part_ref.shape[1]
    order = mine_ref.shape[0] - 8
    me = lax.axis_index("x_hi")
    total = None
    for which, both in enumerate((mine_ref, other_ref)):
        for group in range(groups):
            own = slice(group * per, (group + 1) * per)
            source = 2 * group + (1 - me if which else me)
            held[which, own, 0:LANES] = grad_ref[source, 0:per, :]
            held[which, own, LANES:] = grad_ref[source, per : 2 * per, :]
        decay = decay_of(both[order : order + 1, :], tap_rows, taps)
        left_high, left_low = two_terms(both[0:order, :])
        high, low = two_terms(decay * held[which])
        term = dot(left_high, high) + dot(left_high, low) + dot(left_low, high)
        total = term if total is None else total + term
    part_ref[...] = total


def finish_kernel(recv_ref, grad_ref, near_ref, far_ref, x_ref, filter_ref, feature_ref, rows):
    groups, span = recv_ref.shape[:2]
    per = grad_ref.shape[1] // 2
    channels = x_ref.shape[0]
    subs = x_ref.shape[1] // SUB
    me = lax.axis_index("x_hi")
    feature_ref[...] = near_ref[...] + far_ref[...]
    for group in range(groups):
        own = slice(group * per, (group + 1) * per)
        filter_ref[own, 0:LANES] = grad_ref[2 * group + me, 0:per, :]
        filter_ref[own, LANES:] = grad_ref[2 * group + me, per : 2 * per, :]
        block = recv_ref[group].astype(F32)
        for half in range(2):
            rows[half, group * span : (group + 1) * span, :] = block[:, half * LANES : (half + 1) * LANES]
    for sub in range(subs):
        for half in range(2):
            start = sub * SUB + half * LANES
            x_ref[:, start : start + LANES] = rows[half, pl.ds(sub, channels, stride=subs), :].astype(BF16)


def call(kernel, out, scratch, flops, fetched=(), limit=VMEM_LIMIT):
    scratch_shapes = [pltpu.VMEM(shape, F32) for shape in scratch]
    specs = {}
    if fetched:
        scratch_shapes += [pltpu.VMEM(value.shape, value.dtype) for value in fetched]
        scratch_shapes.append(pltpu.SemaphoreType.DMA((len(fetched),)))
        specs["in_specs"] = [pl.BlockSpec(memory_space=pltpu.HBM)] * len(fetched)
    return pl.pallas_call(
        kernel,
        out_shape=out,
        scratch_shapes=scratch_shapes,
        **specs,
        compiler_params=pltpu.CompilerParams(vmem_limit_bytes=limit),
        cost_estimate=pl.CostEstimate(flops=flops, bytes_accessed=1 << 20, transcendentals=0),
    )


def swapped(values, axis, mask):
    return lax.ppermute(values, axis, [(i, i ^ mask) for i in range(lax.axis_size(axis))])


def paired(values, axis, partner):
    return lax.ppermute(values, axis, list(enumerate(partner)))


FAR = (6, 7, 4, 5, 2, 3, 0, 1)


def halves_of_sum(values, axis):
    near = [swapped(values, axis, mask) for mask in (1, 2, 3)]
    values = values + near[0] + near[1] + near[2]
    return values, paired(values, axis, FAR)


def shards(inputs, cotangent, features, projection, decay_rates):
    channels, block_len = inputs.shape
    tap_rows = features.shape[1]
    groups = lax.axis_size("ctx")
    per = channels // groups
    subs = block_len // SUB
    taps = 2 * block_len
    lags = taps // SUB
    shape = jax.ShapeDtypeStruct
    forward, backward = dft_tables()

    def exchanged(values, axes):
        return lax.all_to_all(values, axes, 0, 0, tiled=True)

    order = projection.shape[0]
    payload, both = call(
        lambda *refs: pack_kernel(groups, taps, *refs),
        (shape((groups, 144, LANES), BF16), shape((order + 8, channels), F32)),
        [(4, channels * subs, LANES), (groups, 16, LANES)],
        1 << 22,
        (features, projection, decay_rates.reshape(1, channels), cotangent, inputs),
        60 * 1024 * 1024,
    )(features, projection, decay_rates.reshape(1, channels), cotangent, inputs)
    other = lax.ppermute(both, "x_hi", [(0, 1), (1, 0)])
    received, other = lax.optimization_barrier((exchanged(payload, "ctx"), other))
    blocks = groups * subs
    mixed = (2 * per, 2, blocks + lags, LANES)
    windows, tap_grads = call(
        taps_kernel,
        (shape((2 * per, 2, blocks + lags, LANES), F32), shape((2 * groups, 2 * per, LANES), F32)),
        [(per, 4, blocks + subs, LANES), (6 * per, blocks, LANES), mixed, (6 * per, lags * subs, LANES), (4, per * lags, LANES)],
        1 << 32,
    )(received, forward, backward)
    tap_grads = exchanged(tap_grads, ("ctx", "x_hi"))
    x_parts = call(
        inputs_kernel,
        shape((groups, per * subs, SUB), BF16),
        [(groups * 16, LANES), (6 * per, lags, LANES), mixed, (6 * per, blocks, LANES)],
        1 << 32,
    )(received, windows, forward, backward)
    tap_grads, x_parts = lax.optimization_barrier((tap_grads, x_parts))
    part = call(
        lambda *refs: features_kernel(taps, *refs),
        shape((order, tap_rows), F32),
        [(2, channels, tap_rows)],
        1 << 22,
    )(tap_grads, both, other)
    part, x_parts = lax.optimization_barrier((part, x_parts))
    near, far = halves_of_sum(part, "z")
    return call(
        finish_kernel,
        (shape((channels, block_len), BF16), shape((channels, tap_rows), F32), shape((order, tap_rows), F32)),
        [(2, channels * subs, LANES)],
        1 << 22,
    )(exchanged(x_parts, "ctx"), tap_grads, near, far)


def solution(mesh):
    whole = mesh.shape["ch"]
    mesh = Mesh(mesh.devices.reshape(mesh.shape["ctx"], 2, whole // 2), ("ctx", "x_hi", "z"))
    split = ("x_hi", "z")
    placed = (P(split, "ctx"), P(split, "ctx"), P(None, "ctx"), P(None, split), P(split))
    return jax.shard_map(
        shards,
        mesh=mesh,
        in_specs=placed,
        out_specs=(P(split, "ctx"), P(split, "ctx"), P(None, "ctx")),
        check_vma=False,
    )
```

```python
import math

import jax
import jax.numpy as jnp
import numpy as np
from jax import lax
from jax.experimental import pallas as pl
from jax.experimental.pallas import tpu as pltpu
from jax.sharding import Mesh
from jax.sharding import PartitionSpec as P

SUB = 256
LANES = 128
F32 = jnp.float32
BF16 = jnp.bfloat16
VMEM_LIMIT = 40 * 1024 * 1024


def dft_tables():
    order = np.concatenate([np.arange(0, SUB, 2), np.arange(1, SUB, 2)])
    angles = 2.0 * np.pi * np.arange(SUB)[:, None] * (order[None, :] + 0.5) / (2 * SUB)
    forward = np.concatenate([np.cos(angles), -np.sin(angles)], axis=1)
    pair = []
    for table in (forward, forward.T / SUB):
        high = table.astype(jnp.bfloat16)
        low = (table - high.astype(np.float64)).astype(jnp.bfloat16)
        pair.append(jnp.asarray(np.stack([high, low])))
    return pair


def dot(left, right):
    return jnp.dot(left, right, preferred_element_type=F32)


def two_terms(values):
    high = values.astype(BF16)
    return high, (values - high.astype(F32)).astype(BF16)


def dot_terms(values, table):
    high, low = two_terms(values)
    return dot(high, table[0]) + dot(high, table[1]) + dot(low, table[0])


def decay_of(rates, tap_rows, taps):
    channels = rates.shape[1]
    first = lax.axis_index("ctx") * tap_rows
    positions = (first + lax.broadcasted_iota(jnp.int32, (1, tap_rows), 1)).astype(F32)
    across = lax.broadcasted_iota(jnp.int32, (channels, channels), 1)
    diagonal = lax.broadcasted_iota(jnp.int32, (channels, channels), 0) == across
    column = jnp.sum(jnp.where(diagonal, rates, 0.0), axis=1, keepdims=True)
    return jnp.exp(-column * (positions / taps))


def pack_kernel(groups, taps, *refs):
    sources, (pay_ref, both_ref, rows, frows), held, sems = refs[:5], refs[5:9], refs[9:14], refs[14]
    copies = [pltpu.make_async_copy(src, dst, sems.at[i]) for i, (src, dst) in enumerate(zip(sources, held))]
    for copy in copies:
        copy.start()
    feat_ref, proj_ref, rate_ref, cot_ref, in_ref = held
    channels, block_len = cot_ref.shape
    for copy in copies[:3]:
        copy.wait()
    per = channels // groups
    subs = block_len // SUB
    span = per * subs
    decay = decay_of(rate_ref[...], feat_ref.shape[1], taps)
    order = proj_ref.shape[0]
    both_ref[0:order, :] = proj_ref[...]
    both_ref[order:, :] = jnp.broadcast_to(rate_ref[...], (8, channels))
    product = lax.dot_general(
        proj_ref[...],
        feat_ref[...],
        (((0,), (0,)), ((), ())),
        precision=lax.Precision.HIGHEST,
        preferred_element_type=F32,
    )
    high, low = two_terms(decay * product)
    high = high.astype(F32)
    low = low.astype(F32)
    for group in range(groups):
        own = slice(group * per, (group + 1) * per)
        for half in range(2):
            lanes = slice(half * LANES, (half + 1) * LANES)
            base = half * 2 * per
            frows[group, base : base + per, :] = high[own, lanes]
            frows[group, base + per : base + 2 * per, :] = low[own, lanes]
    pay_ref[:, 4 * span :, :] = frows[...].astype(BF16)
    for which, ref in enumerate((cot_ref, in_ref)):
        copies[3 + which].wait()
        for sub in range(subs):
            for half in range(2):
                start = sub * SUB + half * LANES
                rows[2 * which + half, pl.ds(sub, channels, stride=subs), :] = ref[:, start : start + LANES].astype(F32)
    for part in range(4):
        for group in range(groups):
            pay_ref[group, part * span : (part + 1) * span, :] = rows[part, group * span : (group + 1) * span, :].astype(BF16)


def block_spectra(recv_ref, base, table_ref, store):
    groups = recv_ref.shape[0]
    span = 32
    per, subs = 4, 8
    step = 4
    for first in range(0, groups, step):
        halves = [
            recv_ref[first : first + step, base + half * span : base + (half + 1) * span, :].reshape(step * span, LANES)
            for half in range(2)
        ]
        left = jnp.concatenate(halves, axis=1)
        result = dot(left, table_ref[0]) + dot(left, table_ref[1])
        for src in range(step):
            for chan in range(per):
                row = (src * per + chan) * subs
                for tile in range(4):
                    store(chan, tile, (first + src) * subs, result[row : row + subs, tile * LANES : (tile + 1) * LANES])


def products(real, imag):
    return real - imag, real, imag


def window_of(win_ref, mixed, index, which, row, rows):
    if which == 0:
        return win_ref[index, 0, row : row + rows, :]
    return mixed[index, which - 1, row : row + rows, :]


def taps_kernel(recv_ref, fwd_ref, inv_ref, win_ref, grad_ref, cot_spec, in_spec, mixed, sums, spec):
    groups = recv_ref.shape[0]
    per, subs, lags = 4, 8, 16
    blocks = groups * subs

    def store_cot(chan, tile, row, value):
        cot_spec[chan, tile, row : row + subs, :] = value

    def store_in(chan, tile, row, value):
        in_spec[(chan * 2 + tile % 2) * 3 + 1 + tile // 2, row : row + subs, :] = value

    block_spectra(recv_ref, 0, fwd_ref, store_cot)
    cot_spec[:, :, blocks:, :] = jnp.zeros((per, 4, subs, LANES), F32)
    block_spectra(recv_ref, 64, fwd_ref, store_in)
    for ref in (win_ref, mixed):
        ref[:, :, blocks:, :] = jnp.zeros((2 * per, 2, lags, LANES), F32)
    for chan in range(per):
        now = [cot_spec[chan, tile, 0:blocks, :] for tile in range(4)]
        nxt = [cot_spec[chan, tile, 1 : blocks + 1, :] for tile in range(4)]
        parts = ((now[0] + nxt[2], now[2] - nxt[0]), (now[1] - nxt[3], now[3] + nxt[1]))
        for half, (real, imag) in enumerate(parts):
            base = chan * 2 + half
            win_ref[base, 0, 0:blocks, :] = real
            win_ref[base, 1, 0:blocks, :] = imag
            mixed[base, 0, 0:blocks, :] = imag - real
            mixed[base, 1, 0:blocks, :] = real + imag

    for part in range(2 * per):
        in_spec[3 * part] = in_spec[3 * part + 1] - in_spec[3 * part + 2]

    def one(index, carry):
        for which in range(3):
            acc = [None] * lags
            left = None
            for src in range(groups + 1):
                before = left
                if src < groups:
                    left = in_spec[3 * index + which, src * subs : (src + 1) * subs, :]
                for lag in range(subs):
                    row = src * subs + lag
                    window = window_of(win_ref, mixed, index, which, row, subs)
                    if src < groups:
                        acc[lag] = left * window if src == 0 else acc[lag] + left * window
                    if src > 0:
                        far = lag + subs
                        acc[far] = before * window if src == 1 else acc[far] + before * window
            for lag in range(lags):
                sums[3 * index + which, lag * subs : (lag + 1) * subs, :] = acc[lag]
        return carry

    lax.fori_loop(0, 2 * per, one, 0)
    for chan in range(per):
        for half in range(2):
            totals = []
            for which in range(3):
                index = (chan * 2 + half) * 3 + which
                total = sums[index, pl.ds(0, lags, stride=subs), :]
                for sub in range(1, subs):
                    total = total + sums[index, pl.ds(sub, lags, stride=subs), :]
                totals.append(total)
            spec[half, pl.ds(chan, lags, stride=per), :] = totals[0] + totals[2]
            spec[2 + half, pl.ds(chan, lags, stride=per), :] = totals[0] + totals[1]
    left = jnp.concatenate([spec[tile] for tile in range(4)], axis=1)
    result = dot_terms(left, inv_ref)
    for lag in range(lags):
        own = slice(lag * per, (lag + 1) * per)
        for copy in range(2):
            grad_ref[2 * lag + copy, 0:per, :] = result[own, 0:LANES]
            grad_ref[2 * lag + copy, per : 2 * per, :] = result[own, LANES:]


def inputs_kernel(recv_ref, win_ref, fwd_ref, inv_ref, grad_ref, frows, fspec, mixed, spec):
    groups = recv_ref.shape[0]
    per, subs, lags = 4, 8, 16
    frows[...] = recv_ref[:, 128:144, :].astype(F32).reshape(groups * 16, LANES)
    terms = []
    for term in range(2):
        chans = []
        for chan in range(per):
            halves = [frows[pl.ds(half * 2 * per + term * per + chan, lags, stride=16), :] for half in range(2)]
            chans.append(jnp.concatenate(halves, axis=1))
        terms.append(jnp.concatenate(chans, axis=0).astype(BF16))
    result = dot(terms[0], fwd_ref[0]) + dot(terms[0], fwd_ref[1]) + dot(terms[1], fwd_ref[0])
    for chan in range(per):
        rows = result[chan * lags : (chan + 1) * lags]
        for half in range(2):
            real = rows[:, half * LANES : (half + 1) * LANES]
            imag = rows[:, (2 + half) * LANES : (3 + half) * LANES]
            for which, value in enumerate(products(real, imag)):
                fspec[(chan * 2 + half) * 3 + which] = value

    for part in range(2 * per):
        mixed[part, 0] = win_ref[part, 1] - win_ref[part, 0]
        mixed[part, 1] = win_ref[part, 0] + win_ref[part, 1]

    def one(index, carry):
        for which in range(3):
            own = 3 * index + which
            filt = [jnp.broadcast_to(fspec[own, lag : lag + 1, :], (subs, LANES)) for lag in range(lags)]
            low = None
            for src in range(groups + 1):
                before = low
                near = [None, None]
                far = [None, None]
                for lag in range(subs):
                    row = src * subs + lag
                    window = window_of(win_ref, mixed, index, which, row, subs)
                    way = lag % 2
                    if src < groups:
                        term = filt[lag] * window
                        near[way] = term if near[way] is None else near[way] + term
                    if src > 0:
                        term = filt[lag + subs] * window
                        far[way] = term if far[way] is None else far[way] + term
                if src < groups:
                    low = near[0] + near[1]
                if src > 0:
                    spec[own, (src - 1) * subs : src * subs, :] = before + (far[0] + far[1])
        return carry

    lax.fori_loop(0, 2 * per, one, 0)
    for first in range(0, per, 2):
        pair = []
        for chan in (first, first + 1):
            base = chan * 6
            tiles = [spec[base + 3 * half] + spec[base + 3 * half + 2] for half in range(2)]
            tiles += [spec[base + 3 * half] + spec[base + 3 * half + 1] for half in range(2)]
            pair.append(dot_terms(jnp.concatenate(tiles, axis=1), inv_ref).reshape(groups, subs, SUB))
        both = jnp.concatenate(pair, axis=1)
        grad_ref[:, first * subs : (first + 2) * subs, :] = both.astype(BF16)


def features_kernel(taps, grad_ref, mine_ref, other_ref, part_ref, held):
    groups = grad_ref.shape[0] // 2
    per = grad_ref.shape[1] // 2
    tap_rows = part_ref.shape[1]
    order = mine_ref.shape[0] - 8
    me = lax.axis_index("x_hi")
    total = None
    for which, both in enumerate((mine_ref, other_ref)):
        for group in range(groups):
            own = slice(group * per, (group + 1) * per)
            source = 2 * group + (1 - me if which else me)
            held[which, own, 0:LANES] = grad_ref[source, 0:per, :]
            held[which, own, LANES:] = grad_ref[source, per : 2 * per, :]
        decay = decay_of(both[order : order + 1, :], tap_rows, taps)
        left_high, left_low = two_terms(both[0:order, :])
        high, low = two_terms(decay * held[which])
        term = dot(left_high, high) + dot(left_high, low) + dot(left_low, high)
        total = term if total is None else total + term
    part_ref[...] = total


def finish_kernel(recv_ref, grad_ref, near_ref, far_ref, x_ref, filter_ref, feature_ref, rows):
    groups, span = recv_ref.shape[:2]
    per = grad_ref.shape[1] // 2
    channels = x_ref.shape[0]
    subs = x_ref.shape[1] // SUB
    me = lax.axis_index("x_hi")
    feature_ref[...] = near_ref[...] + far_ref[...]
    for group in range(groups):
        own = slice(group * per, (group + 1) * per)
        filter_ref[own, 0:LANES] = grad_ref[2 * group + me, 0:per, :]
        filter_ref[own, LANES:] = grad_ref[2 * group + me, per : 2 * per, :]
        block = recv_ref[group].astype(F32)
        for half in range(2):
            rows[half, group * span : (group + 1) * span, :] = block[:, half * LANES : (half + 1) * LANES]
    for sub in range(subs):
        for half in range(2):
            start = sub * SUB + half * LANES
            x_ref[:, start : start + LANES] = rows[half, pl.ds(sub, channels, stride=subs), :].astype(BF16)


def call(kernel, out, scratch, flops, fetched=(), limit=VMEM_LIMIT):
    scratch_shapes = [pltpu.VMEM(shape, F32) for shape in scratch]
    specs = {}
    if fetched:
        scratch_shapes += [pltpu.VMEM(value.shape, value.dtype) for value in fetched]
        scratch_shapes.append(pltpu.SemaphoreType.DMA((len(fetched),)))
        specs["in_specs"] = [pl.BlockSpec(memory_space=pltpu.HBM)] * len(fetched)
    return pl.pallas_call(
        kernel,
        out_shape=out,
        scratch_shapes=scratch_shapes,
        **specs,
        compiler_params=pltpu.CompilerParams(vmem_limit_bytes=limit),
        cost_estimate=pl.CostEstimate(flops=flops, bytes_accessed=1 << 20, transcendentals=0),
    )


def swapped(values, axis, mask):
    return lax.ppermute(values, axis, [(i, i ^ mask) for i in range(lax.axis_size(axis))])


def paired(values, axis, partner):
    return lax.ppermute(values, axis, list(enumerate(partner)))


FAR = (6, 7, 4, 5, 2, 3, 0, 1)


def halves_of_sum(values, axis):
    near = [swapped(values, axis, mask) for mask in (1, 2, 3)]
    values = values + near[0] + near[1] + near[2]
    return values, paired(values, axis, FAR)


def shards(inputs, cotangent, features, projection, decay_rates):
    channels, block_len = inputs.shape
    tap_rows = features.shape[1]
    groups = lax.axis_size("ctx")
    per = channels // groups
    subs = block_len // SUB
    taps = 2 * block_len
    lags = taps // SUB
    shape = jax.ShapeDtypeStruct
    forward, backward = dft_tables()

    def exchanged(values, axes):
        return lax.all_to_all(values, axes, 0, 0, tiled=True)

    order = projection.shape[0]
    payload, both = call(
        lambda *refs: pack_kernel(groups, taps, *refs),
        (shape((groups, 144, LANES), BF16), shape((order + 8, channels), F32)),
        [(4, channels * subs, LANES), (groups, 16, LANES)],
        1 << 22,
        (features, projection, decay_rates.reshape(1, channels), cotangent, inputs),
        60 * 1024 * 1024,
    )(features, projection, decay_rates.reshape(1, channels), cotangent, inputs)
    received = exchanged(payload, "ctx")
    blocks = groups * subs
    mixed = (2 * per, 2, blocks + lags, LANES)
    windows, tap_grads = call(
        taps_kernel,
        (shape((2 * per, 2, blocks + lags, LANES), F32), shape((2 * groups, 2 * per, LANES), F32)),
        [(per, 4, blocks + subs, LANES), (6 * per, blocks, LANES), mixed, (6 * per, lags * subs, LANES), (4, per * lags, LANES)],
        1 << 32,
    )(received, forward, backward)
    tap_grads, both = lax.optimization_barrier((tap_grads, both))
    other = lax.ppermute(both, "x_hi", [(0, 1), (1, 0)])
    tap_grads = exchanged(tap_grads, ("ctx", "x_hi"))
    x_parts = call(
        inputs_kernel,
        shape((groups, per * subs, SUB), BF16),
        [(groups * 16, LANES), (6 * per, lags, LANES), mixed, (6 * per, blocks, LANES)],
        1 << 32,
    )(received, windows, forward, backward)
    tap_grads, x_parts, other = lax.optimization_barrier((tap_grads, x_parts, other))
    part = call(
        lambda *refs: features_kernel(taps, *refs),
        shape((order, tap_rows), F32),
        [(2, channels, tap_rows)],
        1 << 22,
    )(tap_grads, both, other)
    part, x_parts = lax.optimization_barrier((part, x_parts))
    near, far = halves_of_sum(part, "z")
    return call(
        finish_kernel,
        (shape((channels, block_len), BF16), shape((channels, tap_rows), F32), shape((order, tap_rows), F32)),
        [(2, channels * subs, LANES)],
        1 << 22,
    )(exchanged(x_parts, "ctx"), tap_grads, near, far)


def solution(mesh):
    whole = mesh.shape["ch"]
    mesh = Mesh(mesh.devices.reshape(mesh.shape["ctx"], 2, whole // 2), ("ctx", "x_hi", "z"))
    split = ("x_hi", "z")
    placed = (P(split, "ctx"), P(split, "ctx"), P(None, "ctx"), P(None, split), P(split))
    return jax.shard_map(
        shards,
        mesh=mesh,
        in_specs=placed,
        out_specs=(P(split, "ctx"), P(split, "ctx"), P(None, "ctx")),
        check_vma=False,
    )
```

```python
import math

import jax
import jax.numpy as jnp
import numpy as np
from jax import lax
from jax.experimental import pallas as pl
from jax.experimental.pallas import tpu as pltpu
from jax.sharding import Mesh
from jax.sharding import PartitionSpec as P

SUB = 256
LANES = 128
F32 = jnp.float32
BF16 = jnp.bfloat16
VMEM_LIMIT = 40 * 1024 * 1024


def dft_tables():
    order = np.concatenate([np.arange(0, SUB, 2), np.arange(1, SUB, 2)])
    angles = 2.0 * np.pi * np.arange(SUB)[:, None] * (order[None, :] + 0.5) / (2 * SUB)
    forward = np.concatenate([np.cos(angles), -np.sin(angles)], axis=1)
    pair = []
    for table in (forward, forward.T / SUB):
        high = table.astype(jnp.bfloat16)
        low = (table - high.astype(np.float64)).astype(jnp.bfloat16)
        pair.append(jnp.asarray(np.stack([high, low])))
    return pair


def dot(left, right):
    return jnp.dot(left, right, preferred_element_type=F32)


def two_terms(values):
    high = values.astype(BF16)
    return high, (values - high.astype(F32)).astype(BF16)


def dot_terms(values, table):
    high, low = two_terms(values)
    both = table[...]
    terms = both.reshape(both.shape[0] * both.shape[1], both.shape[2])
    return dot(jnp.concatenate([high, high], axis=1), terms) + dot(low, table[0])


def decay_of(rates, tap_rows, taps):
    channels = rates.shape[1]
    first = lax.axis_index("ctx") * tap_rows
    positions = (first + lax.broadcasted_iota(jnp.int32, (1, tap_rows), 1)).astype(F32)
    across = lax.broadcasted_iota(jnp.int32, (channels, channels), 1)
    diagonal = lax.broadcasted_iota(jnp.int32, (channels, channels), 0) == across
    column = jnp.sum(jnp.where(diagonal, rates, 0.0), axis=1, keepdims=True)
    return jnp.exp(-column * (positions / taps))


def pack_kernel(groups, taps, *refs):
    sources, (pay_ref, both_ref, rows, frows), held, sems = refs[:5], refs[5:9], refs[9:14], refs[14]
    copies = [pltpu.make_async_copy(src, dst, sems.at[i]) for i, (src, dst) in enumerate(zip(sources, held))]
    for copy in copies:
        copy.start()
    feat_ref, proj_ref, rate_ref, cot_ref, in_ref = held
    channels, block_len = cot_ref.shape
    for copy in copies[:3]:
        copy.wait()
    per = channels // groups
    subs = block_len // SUB
    span = per * subs
    decay = decay_of(rate_ref[...], feat_ref.shape[1], taps)
    order = proj_ref.shape[0]
    both_ref[0:order, :] = proj_ref[...]
    both_ref[order:, :] = jnp.broadcast_to(rate_ref[...], (8, channels))
    product = lax.dot_general(
        proj_ref[...],
        feat_ref[...],
        (((0,), (0,)), ((), ())),
        precision=lax.Precision.HIGHEST,
        preferred_element_type=F32,
    )
    high, low = two_terms(decay * product)
    high = high.astype(F32)
    low = low.astype(F32)
    for group in range(groups):
        own = slice(group * per, (group + 1) * per)
        for half in range(2):
            lanes = slice(half * LANES, (half + 1) * LANES)
            base = half * 2 * per
            frows[group, base : base + per, :] = high[own, lanes]
            frows[group, base + per : base + 2 * per, :] = low[own, lanes]
    pay_ref[:, 4 * span :, :] = frows[...].astype(BF16)
    for which, ref in enumerate((cot_ref, in_ref)):
        copies[3 + which].wait()
        for sub in range(subs):
            for half in range(2):
                start = sub * SUB + half * LANES
                rows[2 * which + half, pl.ds(sub, channels, stride=subs), :] = ref[:, start : start + LANES].astype(F32)
    for part in range(4):
        for group in range(groups):
            pay_ref[group, part * span : (part + 1) * span, :] = rows[part, group * span : (group + 1) * span, :].astype(BF16)


def block_spectra(recv_ref, base, table_ref, store):
    groups = recv_ref.shape[0]
    span = 32
    per, subs = 4, 8
    step = 4
    for first in range(0, groups, step):
        halves = [
            recv_ref[first : first + step, base + half * span : base + (half + 1) * span, :].reshape(step * span, LANES)
            for half in range(2)
        ]
        left = jnp.concatenate(halves, axis=1)
        pair = jnp.concatenate([left, left], axis=1)
        result = dot(pair, table_ref[...].reshape(2 * SUB, 2 * SUB))
        for src in range(step):
            for chan in range(per):
                row = (src * per + chan) * subs
                for tile in range(4):
                    store(chan, tile, (first + src) * subs, result[row : row + subs, tile * LANES : (tile + 1) * LANES])


def products(real, imag):
    return real - imag, real, imag


def window_of(win_ref, mixed, index, which, row, rows):
    if which == 0:
        return win_ref[index, 0, row : row + rows, :]
    return mixed[index, which - 1, row : row + rows, :]


def taps_kernel(recv_ref, fwd_ref, inv_ref, win_ref, grad_ref, cot_spec, in_spec, mixed, sums, spec):
    groups = recv_ref.shape[0]
    per, subs, lags = 4, 8, 16
    blocks = groups * subs

    def store_cot(chan, tile, row, value):
        cot_spec[chan, tile, row : row + subs, :] = value

    def store_in(chan, tile, row, value):
        in_spec[(chan * 2 + tile % 2) * 3 + 1 + tile // 2, row : row + subs, :] = value

    block_spectra(recv_ref, 0, fwd_ref, store_cot)
    cot_spec[:, :, blocks:, :] = jnp.zeros((per, 4, subs, LANES), F32)
    block_spectra(recv_ref, 64, fwd_ref, store_in)
    for ref in (win_ref, mixed):
        ref[:, :, blocks:, :] = jnp.zeros((2 * per, 2, lags, LANES), F32)
    for chan in range(per):
        now = [cot_spec[chan, tile, 0:blocks, :] for tile in range(4)]
        nxt = [cot_spec[chan, tile, 1 : blocks + 1, :] for tile in range(4)]
        parts = ((now[0] + nxt[2], now[2] - nxt[0]), (now[1] - nxt[3], now[3] + nxt[1]))
        for half, (real, imag) in enumerate(parts):
            base = chan * 2 + half
            win_ref[base, 0, 0:blocks, :] = real
            win_ref[base, 1, 0:blocks, :] = imag
            mixed[base, 0, 0:blocks, :] = imag - real
            mixed[base, 1, 0:blocks, :] = real + imag

    for part in range(2 * per):
        in_spec[3 * part] = in_spec[3 * part + 1] - in_spec[3 * part + 2]

    def one(index, carry):
        for which in range(3):
            acc = [None] * lags
            left = None
            for src in range(groups + 1):
                before = left
                if src < groups:
                    left = in_spec[3 * index + which, src * subs : (src + 1) * subs, :]
                for lag in range(subs):
                    row = src * subs + lag
                    window = window_of(win_ref, mixed, index, which, row, subs)
                    if src < groups:
                        acc[lag] = left * window if src == 0 else acc[lag] + left * window
                    if src > 0:
                        far = lag + subs
                        acc[far] = before * window if src == 1 else acc[far] + before * window
            for lag in range(lags):
                sums[3 * index + which, lag * subs : (lag + 1) * subs, :] = acc[lag]
        return carry

    lax.fori_loop(0, 2 * per, one, 0)
    for chan in range(per):
        for half in range(2):
            totals = []
            for which in range(3):
                index = (chan * 2 + half) * 3 + which
                total = sums[index, pl.ds(0, lags, stride=subs), :]
                for sub in range(1, subs):
                    total = total + sums[index, pl.ds(sub, lags, stride=subs), :]
                totals.append(total)
            spec[half, pl.ds(chan, lags, stride=per), :] = totals[0] + totals[2]
            spec[2 + half, pl.ds(chan, lags, stride=per), :] = totals[0] + totals[1]
    left = jnp.concatenate([spec[tile] for tile in range(4)], axis=1)
    result = dot_terms(left, inv_ref)
    for lag in range(lags):
        own = slice(lag * per, (lag + 1) * per)
        for copy in range(2):
            grad_ref[copy * lags + lag, 0:per, :] = result[own, 0:LANES]
            grad_ref[copy * lags + lag, per : 2 * per, :] = result[own, LANES:]


def inputs_kernel(recv_ref, win_ref, fwd_ref, inv_ref, grad_ref, frows, fspec, mixed, spec):
    groups = recv_ref.shape[0]
    per, subs, lags = 4, 8, 16
    frows[...] = recv_ref[:, 128:144, :].astype(F32).reshape(groups * 16, LANES)
    terms = []
    for term in range(2):
        chans = []
        for chan in range(per):
            halves = [frows[pl.ds(half * 2 * per + term * per + chan, lags, stride=16), :] for half in range(2)]
            chans.append(jnp.concatenate(halves, axis=1))
        terms.append(jnp.concatenate(chans, axis=0).astype(BF16))
    result = dot(terms[0], fwd_ref[0]) + dot(terms[0], fwd_ref[1]) + dot(terms[1], fwd_ref[0])
    for chan in range(per):
        rows = result[chan * lags : (chan + 1) * lags]
        for half in range(2):
            real = rows[:, half * LANES : (half + 1) * LANES]
            imag = rows[:, (2 + half) * LANES : (3 + half) * LANES]
            for which, value in enumerate(products(real, imag)):
                fspec[(chan * 2 + half) * 3 + which] = value

    for part in range(2 * per):
        mixed[part, 0] = win_ref[part, 1] - win_ref[part, 0]
        mixed[part, 1] = win_ref[part, 0] + win_ref[part, 1]

    def one(index, carry):
        for which in range(3):
            own = 3 * index + which
            filt = [jnp.broadcast_to(fspec[own, lag : lag + 1, :], (subs, LANES)) for lag in range(lags)]
            low = None
            for src in range(groups + 1):
                before = low
                near = [None, None]
                far = [None, None]
                for lag in range(subs):
                    row = src * subs + lag
                    window = window_of(win_ref, mixed, index, which, row, subs)
                    way = lag % 2
                    if src < groups:
                        term = filt[lag] * window
                        near[way] = term if near[way] is None else near[way] + term
                    if src > 0:
                        term = filt[lag + subs] * window
                        far[way] = term if far[way] is None else far[way] + term
                if src < groups:
                    low = near[0] + near[1]
                if src > 0:
                    spec[own, (src - 1) * subs : src * subs, :] = before + (far[0] + far[1])
        return carry

    lax.fori_loop(0, 2 * per, one, 0)
    for first in range(0, per, 2):
        pair = []
        for chan in (first, first + 1):
            base = chan * 6
            tiles = [spec[base + 3 * half] + spec[base + 3 * half + 2] for half in range(2)]
            tiles += [spec[base + 3 * half] + spec[base + 3 * half + 1] for half in range(2)]
            pair.append(dot_terms(jnp.concatenate(tiles, axis=1), inv_ref).reshape(groups, subs, SUB))
        both = jnp.concatenate(pair, axis=1)
        grad_ref[:, first * subs : (first + 2) * subs, :] = both.astype(BF16)


def features_kernel(taps, grad_ref, mine_ref, other_ref, part_ref, held):
    groups = grad_ref.shape[0] // 2
    per = grad_ref.shape[1] // 2
    tap_rows = part_ref.shape[1]
    order = mine_ref.shape[0] - 8
    me = lax.axis_index("x_hi")
    total = None
    for which, both in enumerate((mine_ref, other_ref)):
        for group in range(groups):
            own = slice(group * per, (group + 1) * per)
            source = groups * (1 - me if which else me) + group
            held[which, own, 0:LANES] = grad_ref[source, 0:per, :]
            held[which, own, LANES:] = grad_ref[source, per : 2 * per, :]
        decay = decay_of(both[order : order + 1, :], tap_rows, taps)
        left_high, left_low = two_terms(both[0:order, :])
        high, low = two_terms(decay * held[which])
        term = dot(left_high, high) + dot(left_high, low) + dot(left_low, high)
        total = term if total is None else total + term
    part_ref[...] = total


def finish_kernel(recv_ref, grad_ref, near_ref, far_ref, x_ref, filter_ref, feature_ref, rows):
    groups, span = recv_ref.shape[:2]
    per = grad_ref.shape[1] // 2
    channels = x_ref.shape[0]
    subs = x_ref.shape[1] // SUB
    me = lax.axis_index("x_hi")
    feature_ref[...] = near_ref[...] + far_ref[...]
    for group in range(groups):
        own = slice(group * per, (group + 1) * per)
        filter_ref[own, 0:LANES] = grad_ref[groups * me + group, 0:per, :]
        filter_ref[own, LANES:] = grad_ref[groups * me + group, per : 2 * per, :]
        block = recv_ref[group].astype(F32)
        for half in range(2):
            rows[half, group * span : (group + 1) * span, :] = block[:, half * LANES : (half + 1) * LANES]
    for sub in range(subs):
        for half in range(2):
            start = sub * SUB + half * LANES
            x_ref[:, start : start + LANES] = rows[half, pl.ds(sub, channels, stride=subs), :].astype(BF16)


def call(kernel, out, scratch, flops, fetched=(), limit=VMEM_LIMIT):
    scratch_shapes = [pltpu.VMEM(shape, F32) for shape in scratch]
    specs = {}
    if fetched:
        scratch_shapes += [pltpu.VMEM(value.shape, value.dtype) for value in fetched]
        scratch_shapes.append(pltpu.SemaphoreType.DMA((len(fetched),)))
        specs["in_specs"] = [pl.BlockSpec(memory_space=pltpu.HBM)] * len(fetched)
    return pl.pallas_call(
        kernel,
        out_shape=out,
        scratch_shapes=scratch_shapes,
        **specs,
        compiler_params=pltpu.CompilerParams(vmem_limit_bytes=limit),
        cost_estimate=pl.CostEstimate(flops=flops, bytes_accessed=1 << 20, transcendentals=0),
    )


def swapped(values, axis, mask):
    return lax.ppermute(values, axis, [(i, i ^ mask) for i in range(lax.axis_size(axis))])


def paired(values, axis, partner):
    return lax.ppermute(values, axis, list(enumerate(partner)))


FAR = (6, 7, 4, 5, 2, 3, 0, 1)


def halves_of_sum(values, axis):
    near = [swapped(values, axis, mask) for mask in (1, 2, 3)]
    values = values + near[0] + near[1] + near[2]
    return values, paired(values, axis, FAR)


def shards(inputs, cotangent, features, projection, decay_rates):
    channels, block_len = inputs.shape
    tap_rows = features.shape[1]
    groups = lax.axis_size("ctx")
    per = channels // groups
    subs = block_len // SUB
    taps = 2 * block_len
    lags = taps // SUB
    shape = jax.ShapeDtypeStruct
    forward, backward = dft_tables()

    def exchanged(values, axes):
        return lax.all_to_all(values, axes, 0, 0, tiled=True)

    order = projection.shape[0]
    payload, both = call(
        lambda *refs: pack_kernel(groups, taps, *refs),
        (shape((groups, 144, LANES), BF16), shape((order + 8, channels), F32)),
        [(4, channels * subs, LANES), (groups, 16, LANES)],
        1 << 22,
        (features, projection, decay_rates.reshape(1, channels), cotangent, inputs),
        60 * 1024 * 1024,
    )(features, projection, decay_rates.reshape(1, channels), cotangent, inputs)
    received = exchanged(payload, "ctx")
    blocks = groups * subs
    mixed = (2 * per, 2, blocks + lags, LANES)
    windows, tap_grads = call(
        taps_kernel,
        (shape((2 * per, 2, blocks + lags, LANES), F32), shape((2 * groups, 2 * per, LANES), F32)),
        [(per, 4, blocks + subs, LANES), (6 * per, blocks, LANES), mixed, (6 * per, lags * subs, LANES), (4, per * lags, LANES)],
        1 << 32,
    )(received, forward, backward)
    tap_grads, both = lax.optimization_barrier((tap_grads, both))
    other = lax.ppermute(both, "x_hi", [(0, 1), (1, 0)])
    tap_grads = exchanged(tap_grads, ("x_hi", "ctx"))
    x_parts = call(
        inputs_kernel,
        shape((groups, per * subs, SUB), BF16),
        [(groups * 16, LANES), (6 * per, lags, LANES), mixed, (6 * per, blocks, LANES)],
        1 << 32,
    )(received, windows, forward, backward)
    tap_grads, x_parts, other = lax.optimization_barrier((tap_grads, x_parts, other))
    part = call(
        lambda *refs: features_kernel(taps, *refs),
        shape((order, tap_rows), F32),
        [(2, channels, tap_rows)],
        1 << 22,
    )(tap_grads, both, other)
    part, x_parts = lax.optimization_barrier((part, x_parts))
    near, far = halves_of_sum(part, "z")
    return call(
        finish_kernel,
        (shape((channels, block_len), BF16), shape((channels, tap_rows), F32), shape((order, tap_rows), F32)),
        [(2, channels * subs, LANES)],
        1 << 22,
    )(exchanged(x_parts, "ctx"), tap_grads, near, far)


def solution(mesh):
    whole = mesh.shape["ch"]
    mesh = Mesh(mesh.devices.reshape(mesh.shape["ctx"], 2, whole // 2), ("ctx", "x_hi", "z"))
    split = ("x_hi", "z")
    placed = (P(split, "ctx"), P(split, "ctx"), P(None, "ctx"), P(None, split), P(split))
    return jax.shard_map(
        shards,
        mesh=mesh,
        in_specs=placed,
        out_specs=(P(split, "ctx"), P(split, "ctx"), P(None, "ctx")),
        check_vma=False,
    )
```

```python
import math

import jax
import jax.numpy as jnp
import numpy as np
from jax import lax
from jax.experimental import pallas as pl
from jax.experimental.pallas import tpu as pltpu
from jax.sharding import Mesh
from jax.sharding import PartitionSpec as P

SUB = 256
LANES = 128
F32 = jnp.float32
BF16 = jnp.bfloat16
VMEM_LIMIT = 40 * 1024 * 1024


def dft_tables():
    order = np.concatenate([np.arange(0, SUB, 2), np.arange(1, SUB, 2)])
    angles = 2.0 * np.pi * np.arange(SUB)[:, None] * (order[None, :] + 0.5) / (2 * SUB)
    forward = np.concatenate([np.cos(angles), -np.sin(angles)], axis=1)
    pair = []
    for table in (forward, forward.T / SUB):
        high = table.astype(jnp.bfloat16)
        low = (table - high.astype(np.float64)).astype(jnp.bfloat16)
        pair.append(jnp.asarray(np.stack([high, low])))
    return pair


def dot(left, right):
    return jnp.dot(left, right, preferred_element_type=F32)


def two_terms(values):
    high = values.astype(BF16)
    return high, (values - high.astype(F32)).astype(BF16)


def dot_terms(values, table):
    high, low = two_terms(values)
    both = table[...]
    terms = both.reshape(both.shape[0] * both.shape[1], both.shape[2])
    return dot(jnp.concatenate([high, high], axis=1), terms) + dot(low, table[0])


def decay_of(rates, tap_rows, taps):
    channels = rates.shape[1]
    first = lax.axis_index("ctx") * tap_rows
    positions = (first + lax.broadcasted_iota(jnp.int32, (1, tap_rows), 1)).astype(F32)
    across = lax.broadcasted_iota(jnp.int32, (channels, channels), 1)
    diagonal = lax.broadcasted_iota(jnp.int32, (channels, channels), 0) == across
    column = jnp.sum(jnp.where(diagonal, rates, 0.0), axis=1, keepdims=True)
    return jnp.exp(-column * (positions / taps))


def pack_kernel(groups, taps, *refs):
    sources, (pay_ref, both_ref, rows, frows), held, sems = refs[:5], refs[5:9], refs[9:14], refs[14]
    copies = [pltpu.make_async_copy(src, dst, sems.at[i]) for i, (src, dst) in enumerate(zip(sources, held))]
    for copy in copies:
        copy.start()
    feat_ref, proj_ref, rate_ref, cot_ref, in_ref = held
    channels, block_len = cot_ref.shape
    for copy in copies[:3]:
        copy.wait()
    per = channels // groups
    subs = block_len // SUB
    span = per * subs
    decay = decay_of(rate_ref[...], feat_ref.shape[1], taps)
    order = proj_ref.shape[0]
    both_ref[0:order, :] = proj_ref[...]
    both_ref[order:, :] = jnp.broadcast_to(rate_ref[...], (8, channels))
    product = lax.dot_general(
        proj_ref[...],
        feat_ref[...],
        (((0,), (0,)), ((), ())),
        precision=lax.Precision.HIGHEST,
        preferred_element_type=F32,
    )
    high, low = two_terms(decay * product)
    high = high.astype(F32)
    low = low.astype(F32)
    for group in range(groups):
        own = slice(group * per, (group + 1) * per)
        for half in range(2):
            lanes = slice(half * LANES, (half + 1) * LANES)
            base = half * 2 * per
            frows[group, base : base + per, :] = high[own, lanes]
            frows[group, base + per : base + 2 * per, :] = low[own, lanes]
    pay_ref[:, 4 * span :, :] = frows[...].astype(BF16)
    for which, ref in enumerate((cot_ref, in_ref)):
        copies[3 + which].wait()
        for sub in range(subs):
            for half in range(2):
                start = sub * SUB + half * LANES
                rows[2 * which + half, pl.ds(sub, channels, stride=subs), :] = ref[:, start : start + LANES].astype(F32)
    for part in range(4):
        for group in range(groups):
            pay_ref[group, part * span : (part + 1) * span, :] = rows[part, group * span : (group + 1) * span, :].astype(BF16)


def block_spectra(recv_ref, base, table_ref, store):
    groups = recv_ref.shape[0]
    span = 32
    per, subs = 4, 8
    step = 4
    for first in range(0, groups, step):
        halves = [
            recv_ref[first : first + step, base + half * span : base + (half + 1) * span, :].reshape(step * span, LANES)
            for half in range(2)
        ]
        left = jnp.concatenate(halves, axis=1)
        pair = jnp.concatenate([left, left], axis=1)
        result = dot(pair, table_ref[...].reshape(2 * SUB, 2 * SUB))
        for src in range(step):
            for chan in range(per):
                row = (src * per + chan) * subs
                for tile in range(4):
                    store(chan, tile, (first + src) * subs, result[row : row + subs, tile * LANES : (tile + 1) * LANES])


def products(real, imag):
    return real - imag, real, imag


def window_of(win_ref, mixed, index, which, row, rows):
    if which == 0:
        return win_ref[index, 0, row : row + rows, :]
    return mixed[index, which - 1, row : row + rows, :]


def taps_kernel(recv_ref, fwd_ref, inv_ref, win_ref, grad_ref, cot_spec, in_spec, mixed, sums, spec):
    groups = recv_ref.shape[0]
    per, subs, lags = 4, 8, 16
    blocks = groups * subs

    def store_cot(chan, tile, row, value):
        cot_spec[chan, tile, row : row + subs, :] = value

    def store_in(chan, tile, row, value):
        in_spec[(chan * 2 + tile % 2) * 3 + 1 + tile // 2, row : row + subs, :] = value

    block_spectra(recv_ref, 0, fwd_ref, store_cot)
    cot_spec[:, :, blocks:, :] = jnp.zeros((per, 4, subs, LANES), F32)
    block_spectra(recv_ref, 64, fwd_ref, store_in)
    for ref in (win_ref, mixed):
        ref[:, :, blocks:, :] = jnp.zeros((2 * per, 2, lags, LANES), F32)
    for chan in range(per):
        now = [cot_spec[chan, tile, 0:blocks, :] for tile in range(4)]
        nxt = [cot_spec[chan, tile, 1 : blocks + 1, :] for tile in range(4)]
        parts = ((now[0] + nxt[2], now[2] - nxt[0]), (now[1] - nxt[3], now[3] + nxt[1]))
        for half, (real, imag) in enumerate(parts):
            base = chan * 2 + half
            win_ref[base, 0, 0:blocks, :] = real
            win_ref[base, 1, 0:blocks, :] = imag
            mixed[base, 0, 0:blocks, :] = imag - real
            mixed[base, 1, 0:blocks, :] = real + imag

    for part in range(2 * per):
        in_spec[3 * part] = in_spec[3 * part + 1] - in_spec[3 * part + 2]

    def one(index, carry):
        for which in range(3):
            acc = [None] * lags
            left = None
            for src in range(groups + 1):
                before = left
                if src < groups:
                    left = in_spec[3 * index + which, src * subs : (src + 1) * subs, :]
                for lag in range(subs):
                    row = src * subs + lag
                    window = window_of(win_ref, mixed, index, which, row, subs)
                    if src < groups:
                        acc[lag] = left * window if src == 0 else acc[lag] + left * window
                    if src > 0:
                        far = lag + subs
                        acc[far] = before * window if src == 1 else acc[far] + before * window
            for lag in range(lags):
                sums[3 * index + which, lag * subs : (lag + 1) * subs, :] = acc[lag]
        return carry

    lax.fori_loop(0, 2 * per, one, 0)
    for chan in range(per):
        for half in range(2):
            totals = []
            for which in range(3):
                index = (chan * 2 + half) * 3 + which
                total = sums[index, pl.ds(0, lags, stride=subs), :]
                for sub in range(1, subs):
                    total = total + sums[index, pl.ds(sub, lags, stride=subs), :]
                totals.append(total)
            spec[half, pl.ds(chan, lags, stride=per), :] = totals[0] + totals[2]
            spec[2 + half, pl.ds(chan, lags, stride=per), :] = totals[0] + totals[1]
    left = jnp.concatenate([spec[tile] for tile in range(4)], axis=1)
    result = dot_terms(left, inv_ref)
    for lag in range(lags):
        own = slice(lag * per, (lag + 1) * per)
        for copy in range(2):
            grad_ref[copy * lags + lag, 0:per, :] = result[own, 0:LANES]
            grad_ref[copy * lags + lag, per : 2 * per, :] = result[own, LANES:]


def inputs_kernel(recv_ref, win_ref, fwd_ref, inv_ref, grad_ref, frows, fspec, mixed, spec):
    groups = recv_ref.shape[0]
    per, subs, lags = 4, 8, 16
    frows[...] = recv_ref[:, 128:144, :].astype(F32).reshape(groups * 16, LANES)
    terms = []
    for term in range(2):
        chans = []
        for chan in range(per):
            halves = [frows[pl.ds(half * 2 * per + term * per + chan, lags, stride=16), :] for half in range(2)]
            chans.append(jnp.concatenate(halves, axis=1))
        terms.append(jnp.concatenate(chans, axis=0).astype(BF16))
    result = dot(terms[0], fwd_ref[0]) + dot(terms[0], fwd_ref[1]) + dot(terms[1], fwd_ref[0])
    for chan in range(per):
        rows = result[chan * lags : (chan + 1) * lags]
        for half in range(2):
            real = rows[:, half * LANES : (half + 1) * LANES]
            imag = rows[:, (2 + half) * LANES : (3 + half) * LANES]
            for which, value in enumerate(products(real, imag)):
                fspec[(chan * 2 + half) * 3 + which] = value

    for part in range(2 * per):
        mixed[part, 0] = win_ref[part, 1] - win_ref[part, 0]
        mixed[part, 1] = win_ref[part, 0] + win_ref[part, 1]

    def one(index, carry):
        for which in range(3):
            own = 3 * index + which
            filt = [jnp.broadcast_to(fspec[own, lag : lag + 1, :], (subs, LANES)) for lag in range(lags)]
            low = None
            for src in range(groups + 1):
                before = low
                near = [None, None]
                far = [None, None]
                for lag in range(subs):
                    row = src * subs + lag
                    window = window_of(win_ref, mixed, index, which, row, subs)
                    way = lag % 2
                    if src < groups:
                        term = filt[lag] * window
                        near[way] = term if near[way] is None else near[way] + term
                    if src > 0:
                        term = filt[lag + subs] * window
                        far[way] = term if far[way] is None else far[way] + term
                if src < groups:
                    low = near[0] + near[1]
                if src > 0:
                    spec[own, (src - 1) * subs : src * subs, :] = before + (far[0] + far[1])
        return carry

    lax.fori_loop(0, 2 * per, one, 0)
    for first in range(0, per, 2):
        pair = []
        for chan in (first, first + 1):
            base = chan * 6
            tiles = [spec[base + 3 * half] + spec[base + 3 * half + 2] for half in range(2)]
            tiles += [spec[base + 3 * half] + spec[base + 3 * half + 1] for half in range(2)]
            pair.append(dot_terms(jnp.concatenate(tiles, axis=1), inv_ref).reshape(groups, subs, SUB))
        both = jnp.concatenate(pair, axis=1)
        grad_ref[:, first * subs : (first + 2) * subs, :] = both.astype(BF16)


def features_kernel(taps, grad_ref, mine_ref, other_ref, part_ref, held):
    groups = grad_ref.shape[0] // 2
    per = grad_ref.shape[1] // 2
    tap_rows = part_ref.shape[1]
    order = mine_ref.shape[0] - 8
    me = lax.axis_index("x_hi")
    total = None
    for which, both in enumerate((mine_ref, other_ref)):
        for group in range(groups):
            own = slice(group * per, (group + 1) * per)
            source = groups * (1 - me if which else me) + group
            held[which, own, 0:LANES] = grad_ref[source, 0:per, :]
            held[which, own, LANES:] = grad_ref[source, per : 2 * per, :]
        decay = decay_of(both[order : order + 1, :], tap_rows, taps)
        left_high, left_low = two_terms(both[0:order, :])
        high, low = two_terms(decay * held[which])
        term = dot(left_high, high) + dot(left_high, low) + dot(left_low, high)
        total = term if total is None else total + term
    part_ref[...] = total


def finish_kernel(recv_ref, grad_ref, near_ref, far_ref, x_ref, filter_ref, feature_ref, rows):
    groups, span = recv_ref.shape[:2]
    per = grad_ref.shape[1] // 2
    channels = x_ref.shape[0]
    subs = x_ref.shape[1] // SUB
    me = lax.axis_index("x_hi")
    feature_ref[...] = near_ref[...] + far_ref[...]
    for group in range(groups):
        own = slice(group * per, (group + 1) * per)
        filter_ref[own, 0:LANES] = grad_ref[groups * me + group, 0:per, :]
        filter_ref[own, LANES:] = grad_ref[groups * me + group, per : 2 * per, :]
        block = recv_ref[group].astype(F32)
        for half in range(2):
            rows[half, group * span : (group + 1) * span, :] = block[:, half * LANES : (half + 1) * LANES]
    for sub in range(subs):
        for half in range(2):
            start = sub * SUB + half * LANES
            x_ref[:, start : start + LANES] = rows[half, pl.ds(sub, channels, stride=subs), :].astype(BF16)


def call(kernel, out, scratch, flops, fetched=(), limit=VMEM_LIMIT):
    scratch_shapes = [pltpu.VMEM(shape, F32) for shape in scratch]
    specs = {}
    if fetched:
        scratch_shapes += [pltpu.VMEM(value.shape, value.dtype) for value in fetched]
        scratch_shapes.append(pltpu.SemaphoreType.DMA((len(fetched),)))
        specs["in_specs"] = [pl.BlockSpec(memory_space=pltpu.HBM)] * len(fetched)
    return pl.pallas_call(
        kernel,
        out_shape=out,
        scratch_shapes=scratch_shapes,
        **specs,
        compiler_params=pltpu.CompilerParams(vmem_limit_bytes=limit),
        cost_estimate=pl.CostEstimate(flops=flops, bytes_accessed=1 << 20, transcendentals=0),
    )


def swapped(values, axis, mask):
    return lax.ppermute(values, axis, [(i, i ^ mask) for i in range(lax.axis_size(axis))])


def paired(values, axis, partner):
    return lax.ppermute(values, axis, list(enumerate(partner)))


FAR = (6, 7, 4, 5, 2, 3, 0, 1)


def halves_of_sum(values, axis):
    near = [swapped(values, axis, mask) for mask in (3, 2, 1)]
    values = values + near[0] + near[1] + near[2]
    return values, paired(values, axis, FAR)


def shards(inputs, cotangent, features, projection, decay_rates):
    channels, block_len = inputs.shape
    tap_rows = features.shape[1]
    groups = lax.axis_size("ctx")
    per = channels // groups
    subs = block_len // SUB
    taps = 2 * block_len
    lags = taps // SUB
    shape = jax.ShapeDtypeStruct
    forward, backward = dft_tables()

    def exchanged(values, axes):
        return lax.all_to_all(values, axes, 0, 0, tiled=True)

    order = projection.shape[0]
    payload, both = call(
        lambda *refs: pack_kernel(groups, taps, *refs),
        (shape((groups, 144, LANES), BF16), shape((order + 8, channels), F32)),
        [(4, channels * subs, LANES), (groups, 16, LANES)],
        1 << 22,
        (features, projection, decay_rates.reshape(1, channels), cotangent, inputs),
        60 * 1024 * 1024,
    )(features, projection, decay_rates.reshape(1, channels), cotangent, inputs)
    received = exchanged(payload, "ctx")
    blocks = groups * subs
    mixed = (2 * per, 2, blocks + lags, LANES)
    windows, tap_grads = call(
        taps_kernel,
        (shape((2 * per, 2, blocks + lags, LANES), F32), shape((2 * groups, 2 * per, LANES), F32)),
        [(per, 4, blocks + subs, LANES), (6 * per, blocks, LANES), mixed, (6 * per, lags * subs, LANES), (4, per * lags, LANES)],
        1 << 32,
    )(received, forward, backward)
    tap_grads, both = lax.optimization_barrier((tap_grads, both))
    other = lax.ppermute(both, "x_hi", [(0, 1), (1, 0)])
    tap_grads = exchanged(tap_grads, ("x_hi", "ctx"))
    x_parts = call(
        inputs_kernel,
        shape((groups, per * subs, SUB), BF16),
        [(groups * 16, LANES), (6 * per, lags, LANES), mixed, (6 * per, blocks, LANES)],
        1 << 32,
    )(received, windows, forward, backward)
    tap_grads, x_parts, other = lax.optimization_barrier((tap_grads, x_parts, other))
    part = call(
        lambda *refs: features_kernel(taps, *refs),
        shape((order, tap_rows), F32),
        [(2, channels, tap_rows)],
        1 << 22,
    )(tap_grads, both, other)
    part, x_parts = lax.optimization_barrier((part, x_parts))
    near, far = halves_of_sum(part, "z")
    return call(
        finish_kernel,
        (shape((channels, block_len), BF16), shape((channels, tap_rows), F32), shape((order, tap_rows), F32)),
        [(2, channels * subs, LANES)],
        1 << 22,
    )(exchanged(x_parts, "ctx"), tap_grads, near, far)


def solution(mesh):
    whole = mesh.shape["ch"]
    mesh = Mesh(mesh.devices.reshape(mesh.shape["ctx"], 2, whole // 2), ("ctx", "x_hi", "z"))
    split = ("x_hi", "z")
    placed = (P(split, "ctx"), P(split, "ctx"), P(None, "ctx"), P(None, split), P(split))
    return jax.shard_map(
        shards,
        mesh=mesh,
        in_specs=placed,
        out_specs=(P(split, "ctx"), P(split, "ctx"), P(None, "ctx")),
        check_vma=False,
    )
```
